32 devices in a mesh: member: 2 (over x), gx: 16 (over z, y, core).
Axes of the slice: x: 2, y: 2, z: 4, core: 2. Of those that a mesh axis runs over, the one named last changes fastest.
Arguments:
- edge_tiles: bfloat16 [128, 832, 832], P('member', 'gx'), parts along dimension 0, may hold values from -0.036771775 to 0.036771775
- trial_panel: float32 [64, 48, 832], P(('member', 'gx')), parts along dimension 0, may hold values from -6 to 6
- col_blocks: int32 [32, 2], replicated, may hold values from 0 to 31, as said below
Outputs:
- filtered_low: float32 [64, 48, 832], P(('member', 'gx')), parts along dimension 0
- filtered_high: float32 [64, 48, 832], P(('member', 'gx')), parts along dimension 0
The draws below stay inside these ranges and needn't reach their ends.
There are 2 independent parts, one for each index of `member`. The reference program is written for one: setup_inputs(seed, part) draws one part's arguments, and reference() takes and returns one part's arrays. A program takes and returns all parts, laid end to end along the dimension named above; an argument that names none is the same for every part. Nothing has to cross between parts.
Inputs may be any that keep to these rules, and one draw needn't show every extreme that they name: Row block b lies in domain b // 2; every col_blocks[b, s] lies in the same domain or in the next one, cyclically, the domain after the last being the first. When b is the first block of its domain, col_blocks[b, 0] lies in the next domain. Row block 30 couples to blocks 0 and 31. Entries may repeat.
All inputs are finite; a program needn't handle non-finite values.
Results may differ from the reference program's by a relative error of at most 0.0034.
Values may be sent and summed in bfloat16 or wider, within the bound.
No kernel may reach another device: no remote copies, remote signals or barrier semaphores. Data moves between devices by JAX's collectives and lax.ppermute only.
A program may use at most 64 MiB of HBM per device.

```python
import jax
import jax.numpy as jnp

ORBS = 832
VECS = 48
BLK_DEV = 2
SLOTS = 2
DEGREE = 4
BLOCKS = 32
EDGES = 64


def draw_edge_tiles(key, part):
    key = jax.random.fold_in(key, 11)
    spread_scale = (16.0 * SLOTS * ORBS) ** (-0.5)
    tile_shape = (EDGES, ORBS, ORBS)
    samples = jnp.clip(jax.random.normal(key, tile_shape, jnp.float32), -6.0, 6.0)
    return (samples * spread_scale).astype(jnp.bfloat16)


def draw_col_blocks(key, part):
    key = jax.random.fold_in(key, 23)
    lead_key, rest_key = jax.random.split(key)
    offsets = jax.random.randint(rest_key, (BLOCKS, SLOTS), 0, 2 * BLK_DEV)
    crossing = jax.random.randint(lead_key, (BLOCKS,), BLK_DEV, 2 * BLK_DEV)
    row_ids = jnp.arange(BLOCKS, dtype=jnp.int32)
    leading = row_ids % BLK_DEV == 0
    offsets = offsets.at[:, 0].set(jnp.where(leading, crossing, offsets[:, 0]))
    final_row = BLOCKS - BLK_DEV
    offsets = offsets.at[final_row, 0].set(BLK_DEV)
    offsets = offsets.at[final_row, 1].set(BLK_DEV - 1)
    domain = row_ids // BLK_DEV
    return ((domain * BLK_DEV)[:, None] + offsets) % BLOCKS


def level_of(stream_key, shape, pieces, low, high):
    def one(axis_at, shards_of):
        heights = jax.random.uniform(jax.random.fold_in(jax.random.fold_in(stream_key, 6), axis_at), (shards_of,), jnp.float32, low / len(pieces), high / len(pieces))
        return jnp.repeat(jnp.exp(heights), shape[axis_at] // shards_of).reshape((-1,) + (1,) * (len(shape) - axis_at - 1))

    gain = one(*pieces[0])
    for cut in pieces[1:]:
        gain = gain * one(*cut)
    return gain


def gaussian(rng, shape, deviation, reach, cuts=(), held_as=jnp.bfloat16):
    level = level_of(rng, shape, cuts, -0.22, 0.18) if cuts else 1.0
    entries = jax.random.normal(rng, shape, jnp.float32) * deviation * level
    return jnp.minimum(jnp.maximum(entries, -reach), reach).astype(held_as)


def setup_inputs(seed: int = 0, part: int = 0) -> dict:
    seeds = jax.random.split(jax.random.key(seed), 4)
    part_keys = jax.random.split(jax.random.fold_in(seeds[3], part), 4)
    return {
        "edge_tiles": draw_edge_tiles(jax.random.fold_in(jax.random.fold_in(seeds[3], part), 71), part),
        "trial_panel": gaussian(part_keys[1], (BLOCKS, VECS, ORBS), 1.0, 6.0, ((0, 16),), jnp.float32),
        "col_blocks": draw_col_blocks(jax.random.fold_in(seeds[3], 71), part),
    }


def apply_hamiltonian(rounded, tile_set, col_blocks):
    values = rounded.astype(jnp.float32)
    picked = values[col_blocks]
    direct = jnp.einsum("bskn,bsmn->bkm", picked, tile_set)
    turned = jnp.einsum("bkm,bsmn->bskn", values, tile_set)
    spread = jnp.zeros(values.shape, jnp.float32).at[col_blocks.reshape(-1)].add(turned.reshape(-1, VECS, ORBS))
    return direct + spread


def reference(edge_tiles, trial_panel, col_blocks):
    tile_set = edge_tiles.astype(jnp.float32).reshape(BLOCKS, SLOTS, ORBS, ORBS)
    previous = trial_panel
    current = apply_hamiltonian(trial_panel.astype(jnp.bfloat16), tile_set, col_blocks)
    for degree_k in range(DEGREE - 1):
        following = 2.0 * apply_hamiltonian(current.astype(jnp.bfloat16), tile_set, col_blocks) - previous
        previous, current = current, following
    return previous, current
```

```python
import functools

import jax
import jax.numpy as jnp
from jax import lax
from jax.experimental import pallas as pl
from jax.experimental.pallas import tpu as pltpu
from jax.sharding import PartitionSpec as P

DEGREE = 4
LANES = 128
QUAD = 4
MIB = 2**20
VMEM_WHOLE = pl.BlockSpec(memory_space=pltpu.VMEM)
HBM_WHOLE = pl.BlockSpec(memory_space=pltpu.HBM)
SMEM_WHOLE = pl.BlockSpec(memory_space=pltpu.SMEM)


def passed_along(value, axis, steps):
    count = lax.axis_size(axis)
    pairs = [(source, (source + steps) % count) for source in range(count)]
    return lax.ppermute(value, axis, pairs)


def dot_nn(a, b):
    return lax.dot_general(a, b, (((1,), (0,)), ((), ())), preferred_element_type=jnp.float32)


def dot_nt(a, b):
    return lax.dot_general(a, b, (((1,), (1,)), ((), ())), preferred_element_type=jnp.float32)


def selector(rows, columns, source_of_row):
    row = lax.broadcasted_iota(jnp.int32, (rows, columns), 0)
    column = lax.broadcasted_iota(jnp.int32, (rows, columns), 1)
    return (column == source_of_row(row)).astype(jnp.bfloat16)


def pack_kernel(batch, x_ref, out_ref, x_buf, out_buf, tail_buf, in_sems, out_sems):
    rows, tiles, orbs = x_ref.shape
    group = tiles // QUAD
    unit = QUAD * QUAD
    steps = rows // QUAD
    full = orbs // LANES
    half = LANES // 2
    length = steps * unit
    arrivals = []
    for j in range(steps):
        part = pl.ds(j * QUAD, QUAD)
        arrivals.append(pltpu.make_async_copy(x_ref.at[part], x_buf.at[part], in_sems.at[j]))
        arrivals[-1].start()
    order = selector(QUAD * tiles, QUAD * tiles, lambda o: ((o % unit) // QUAD) * tiles + (o // unit) * QUAD + o % QUAD)
    leaving = []

    def leave(first, count):
        part = pl.ds(first, count)
        copy = pltpu.make_async_copy(out_buf.at[:, part, :], out_ref.at[:, part, :], out_sems.at[len(leaving)])
        copy.start()
        leaving.append(copy)

    begun = 0
    for j in range(steps):
        arrivals[j].wait()
        data = x_buf[j * QUAD : (j + 1) * QUAD].reshape(QUAD * tiles, orbs)
        for left in range(0, full * LANES, 2 * LANES):
            width = min(2 * LANES, full * LANES - left)
            part = dot_nn(order, data[:, left : left + width]).astype(jnp.bfloat16)
            for k in range(0, width, LANES):
                first = (left + k) // LANES * length + j * unit
                out_buf[:, first : first + unit, :] = part[:, k : k + LANES].reshape(group, unit, LANES)
        last = dot_nn(order, data[:, full * LANES :]).reshape(group, unit, half)
        both = jnp.concatenate([last[:, : unit // 2], last[:, unit // 2 :]], axis=2)
        tail_buf[:, j * unit // 2 : (j + 1) * unit // 2, :] = both
        if (j + 1) % batch == 0 or j == steps - 1:
            for k in range(full):
                leave(k * length + begun * unit, (j + 1 - begun) * unit)
            begun = j + 1
    out_buf[:, full * length :, :] = tail_buf[...].astype(jnp.bfloat16)
    leave(full * length, length // 2)
    for copy in leaving:
        copy.wait()


def pack(edge_tiles):
    tiles, rows, orbs = edge_tiles.shape
    group = tiles // QUAD
    turned = jnp.transpose(edge_tiles, (1, 0, 2))
    flat = rows * QUAD * orbs // LANES
    steps = rows // QUAD
    batch = 4
    copies = -(-steps // batch) * (orbs // LANES) + 1
    return pl.pallas_call(
        functools.partial(pack_kernel, batch),
        out_shape=jax.ShapeDtypeStruct((group, flat, LANES), jnp.bfloat16),
        in_specs=[HBM_WHOLE],
        out_specs=HBM_WHOLE,
        scratch_shapes=[
            pltpu.VMEM((rows, tiles, orbs), jnp.bfloat16),
            pltpu.VMEM((group, flat, LANES), jnp.bfloat16),
            pltpu.VMEM((group, rows * QUAD // 2, LANES), jnp.float32),
            pltpu.SemaphoreType.DMA((steps,)),
            pltpu.SemaphoreType.DMA((copies,)),
        ],
        compiler_params=pltpu.CompilerParams(vmem_limit_bytes=32 * MIB),
        name="pack",
    )(turned)


def unpack_kernel(orbs, in_ref, out_ref, body_ref, tail_ref, sems):
    group, rows, _ = body_ref.shape
    full = orbs // LANES
    half = LANES // 2
    unit = QUAD * QUAD
    copies = [
        pltpu.make_async_copy(
            in_ref.at[:, pl.ds(j * rows, rows), :], body_ref.at[:, :, pl.ds(j * LANES, LANES)], sems.at[j]
        )
        for j in range(full)
    ]
    copies.append(pltpu.make_async_copy(in_ref.at[:, pl.ds(full * rows, rows // 2), :], tail_ref, sems.at[full]))
    for copy in copies:
        copy.start()
    for copy in copies:
        copy.wait()
    block = 4 * QUAD
    size = block * unit
    span = block * QUAD
    order = selector(size, size, lambda o: (o % span) // QUAD * unit + (o % QUAD) * QUAD + o // span)
    order_tail = selector(
        size, size // 2, lambda o: (o % span) // QUAD * (unit // 2) + (o % QUAD) % 2 * QUAD + o // span
    )
    early = lax.broadcasted_iota(jnp.int32, (size, half), 0) % QUAD < 2
    body = body_ref.reshape(group * rows, full * LANES)
    tail = tail_ref.reshape(group * rows // 2, LANES)
    for i in range(orbs // span):
        clean = dot_nn(order, body[pl.ds(i * size, size), :]).astype(jnp.bfloat16)
        both = dot_nn(order_tail, tail[pl.ds(i * size // 2, size // 2), :])
        last = jnp.where(early, both[:, :half], both[:, half:]).astype(jnp.bfloat16)
        for e in range(QUAD):
            out_ref[e, pl.ds(i * span, span), : full * LANES] = clean[e * span : (e + 1) * span]
            out_ref[e, pl.ds(i * span, span), full * LANES :] = last[e * span : (e + 1) * span]


def unpack(arrived, rows, orbs):
    group = arrived.shape[0]
    full = orbs // LANES
    return pl.pallas_call(
        functools.partial(unpack_kernel, orbs),
        out_shape=jax.ShapeDtypeStruct((QUAD, orbs, orbs), jnp.bfloat16),
        in_specs=[HBM_WHOLE],
        out_specs=VMEM_WHOLE,
        scratch_shapes=[
            pltpu.VMEM((group, rows * QUAD, full * LANES), jnp.bfloat16),
            pltpu.VMEM((group, rows * QUAD // 2, LANES), jnp.bfloat16),
            pltpu.SemaphoreType.DMA((full + 1,)),
        ],
        compiler_params=pltpu.CompilerParams(vmem_limit_bytes=32 * MIB),
        name="unpack",
    )(arrived)


def turned_kernel(target_ref, rounded_ref, tiles_ref, own_ref, send_ref, acc_ref):
    blk_dev = rounded_ref.shape[0]
    edges = tiles_ref.shape[0]
    acc_ref[...] = jnp.zeros_like(acc_ref)
    for e in range(edges):
        acc_ref[target_ref[e]] += dot_nn(rounded_ref[e * blk_dev // edges], tiles_ref[e])
    own_ref[...] = acc_ref[:blk_dev]
    send_ref[...] = acc_ref[blk_dev:].astype(jnp.bfloat16)


def turned_terms(target, rounded, tiles):
    blk_dev, vecs, orbs = rounded.shape
    return pl.pallas_call(
        turned_kernel,
        out_shape=(
            jax.ShapeDtypeStruct(rounded.shape, jnp.float32),
            jax.ShapeDtypeStruct(rounded.shape, jnp.bfloat16),
        ),
        in_specs=[SMEM_WHOLE, VMEM_WHOLE, VMEM_WHOLE],
        out_specs=(VMEM_WHOLE, VMEM_WHOLE),
        scratch_shapes=[pltpu.VMEM((2 * blk_dev, vecs, orbs), jnp.float32)],
        compiler_params=pltpu.CompilerParams(vmem_limit_bytes=16 * MIB),
        cost_estimate=pl.CostEstimate(
            flops=2 * tiles.size * vecs * 4, bytes_accessed=2 * tiles.size, transcendentals=0
        ),
        name="turned",
    )(target, rounded, tiles)


def direct_kernel(target_ref, rounded_ref, following_ref, tiles_ref, own_ref, out_ref, picked_ref):
    blk_dev = rounded_ref.shape[0]
    edges = tiles_ref.shape[0]
    slots = edges // blk_dev
    picked_ref[:blk_dev] = rounded_ref[...]
    picked_ref[blk_dev:] = following_ref[...]
    for b in range(blk_dev):
        total = own_ref[b]
        for e in range(b * slots, (b + 1) * slots):
            total += dot_nt(picked_ref[target_ref[e]], tiles_ref[e])
        out_ref[b] = total


def direct_terms(target, rounded, following, tiles, own):
    blk_dev, vecs, orbs = rounded.shape
    return pl.pallas_call(
        direct_kernel,
        out_shape=jax.ShapeDtypeStruct(rounded.shape, jnp.float32),
        in_specs=[SMEM_WHOLE] + [VMEM_WHOLE] * 4,
        out_specs=VMEM_WHOLE,
        scratch_shapes=[pltpu.VMEM((2 * blk_dev, vecs, orbs), jnp.bfloat16)],
        compiler_params=pltpu.CompilerParams(vmem_limit_bytes=16 * MIB),
        cost_estimate=pl.CostEstimate(
            flops=2 * tiles.size * vecs * 4, bytes_accessed=2 * tiles.size, transcendentals=0
        ),
        name="direct",
    )(target, rounded, following, tiles, own)


def gathered_tiles(edge_tiles, block_total, slots):
    group = lax.axis_size("gx")
    tiles, rows, orbs = edge_tiles.shape
    per_owner = tiles // group
    if per_owner == QUAD and rows % QUAD == 0 and orbs % LANES == LANES // 2 and orbs % (4 * QUAD * QUAD) == 0:
        sent = lax.all_to_all(pack(edge_tiles), "gx", split_axis=0, concat_axis=0, tiled=True)
        return unpack(sent, rows, orbs)
    return lax.all_to_all(edge_tiles, "gx", split_axis=0, concat_axis=1, tiled=True)


def per_device(edge_tiles, trial_panel, col_blocks):
    blk_dev, _, _ = trial_panel.shape
    slots = col_blocks.shape[1]
    block_total = blk_dev * lax.axis_size("gx")
    domain = lax.axis_index("gx")
    own_cols = lax.dynamic_slice_in_dim(col_blocks, domain * blk_dev, blk_dev, 0).reshape(-1)
    target = jnp.mod(own_cols - domain * blk_dev, block_total)
    tiles = gathered_tiles(edge_tiles, block_total, slots)

    def operate(rounded):
        following = passed_along(rounded, "gx", -1)
        own, send = turned_terms(target, rounded, tiles)
        arrive = passed_along(send, "gx", 1)
        return direct_terms(target, rounded, following, tiles, own) + arrive.astype(jnp.float32)

    previous = trial_panel
    current = operate(trial_panel.astype(jnp.bfloat16))
    for _ in range(DEGREE - 1):
        following_panel = 2.0 * operate(current.astype(jnp.bfloat16)) - previous
        previous, current = current, following_panel
    return previous, current


def solution(mesh):
    return jax.shard_map(
        per_device,
        mesh=mesh,
        in_specs=(P("member", "gx", None), P(("member", "gx"), None, None), P()),
        out_specs=(P(("member", "gx"), None, None), P(("member", "gx"), None, None)),
        check_vma=False,
    )
```

```python
import functools

import jax
import jax.numpy as jnp
from jax import lax
from jax.experimental import pallas as pl
from jax.experimental.pallas import tpu as pltpu
from jax.sharding import PartitionSpec as P

DEGREE = 4
LANES = 128
QUAD = 4
MIB = 2**20
VMEM_WHOLE = pl.BlockSpec(memory_space=pltpu.VMEM)
HBM_WHOLE = pl.BlockSpec(memory_space=pltpu.HBM)
SMEM_WHOLE = pl.BlockSpec(memory_space=pltpu.SMEM)


def passed_along(value, axis, steps):
    count = lax.axis_size(axis)
    pairs = [(source, (source + steps) % count) for source in range(count)]
    return lax.ppermute(value, axis, pairs)


def dot_nn(a, b):
    return lax.dot_general(a, b, (((1,), (0,)), ((), ())), preferred_element_type=jnp.float32)


def dot_nt(a, b):
    return lax.dot_general(a, b, (((1,), (1,)), ((), ())), preferred_element_type=jnp.float32)


def selector(rows, columns, source_of_row):
    row = lax.broadcasted_iota(jnp.int32, (rows, columns), 0)
    column = lax.broadcasted_iota(jnp.int32, (rows, columns), 1)
    return (column == source_of_row(row)).astype(jnp.bfloat16)


def pack_kernel(batch, x_ref, out_ref, x_buf, out_buf, tail_buf, in_sems, out_sems):
    rows, tiles, orbs = x_ref.shape
    group = tiles // QUAD
    unit = QUAD * QUAD
    steps = rows // QUAD
    full = orbs // LANES
    half = LANES // 2
    length = steps * unit
    arrivals = []
    for j in range(steps):
        part = pl.ds(j * QUAD, QUAD)
        arrivals.append(pltpu.make_async_copy(x_ref.at[part], x_buf.at[part], in_sems.at[j]))
        arrivals[-1].start()
    order = selector(QUAD * tiles, QUAD * tiles, lambda o: ((o % unit) // QUAD) * tiles + (o // unit) * QUAD + o % QUAD)
    leaving = []

    def leave(first, count):
        part = pl.ds(first, count)
        copy = pltpu.make_async_copy(out_buf.at[:, part, :], out_ref.at[:, part, :], out_sems.at[len(leaving)])
        copy.start()
        leaving.append(copy)

    begun = 0
    for j in range(steps):
        arrivals[j].wait()
        data = x_buf[j * QUAD : (j + 1) * QUAD].reshape(QUAD * tiles, orbs)
        for left in range(0, full * LANES, 2 * LANES):
            width = min(2 * LANES, full * LANES - left)
            part = dot_nn(order, data[:, left : left + width]).astype(jnp.bfloat16)
            for k in range(0, width, LANES):
                first = (left + k) // LANES * length + j * unit
                out_buf[:, first : first + unit, :] = part[:, k : k + LANES].reshape(group, unit, LANES)
        last = dot_nn(order, data[:, full * LANES :]).reshape(group, unit, half)
        both = jnp.concatenate([last[:, : unit // 2], last[:, unit // 2 :]], axis=2)
        tail_buf[:, j * unit // 2 : (j + 1) * unit // 2, :] = both
        if (j + 1) % batch == 0 or j == steps - 1:
            for k in range(full):
                leave(k * length + begun * unit, (j + 1 - begun) * unit)
            begun = j + 1
    out_buf[:, full * length :, :] = tail_buf[...].astype(jnp.bfloat16)
    leave(full * length, length // 2)
    for copy in leaving:
        copy.wait()


def pack(edge_tiles):
    tiles, rows, orbs = edge_tiles.shape
    group = tiles // QUAD
    turned = jnp.transpose(edge_tiles, (1, 0, 2))
    flat = rows * QUAD * orbs // LANES
    steps = rows // QUAD
    batch = 4
    copies = -(-steps // batch) * (orbs // LANES) + 1
    return pl.pallas_call(
        functools.partial(pack_kernel, batch),
        out_shape=jax.ShapeDtypeStruct((group, flat, LANES), jnp.bfloat16),
        in_specs=[HBM_WHOLE],
        out_specs=HBM_WHOLE,
        scratch_shapes=[
            pltpu.VMEM((rows, tiles, orbs), jnp.bfloat16),
            pltpu.VMEM((group, flat, LANES), jnp.bfloat16),
            pltpu.VMEM((group, rows * QUAD // 2, LANES), jnp.float32),
            pltpu.SemaphoreType.DMA((steps,)),
            pltpu.SemaphoreType.DMA((copies,)),
        ],
        compiler_params=pltpu.CompilerParams(vmem_limit_bytes=58 * MIB),
        name="pack",
    )(turned)


def unpack_kernel(orbs, in_ref, out_ref, body_ref, tail_ref, sems):
    group, rows, _ = body_ref.shape
    full = orbs // LANES
    half = LANES // 2
    unit = QUAD * QUAD
    copies = [
        pltpu.make_async_copy(
            in_ref.at[:, pl.ds(j * rows, rows), :], body_ref.at[:, :, pl.ds(j * LANES, LANES)], sems.at[j]
        )
        for j in range(full)
    ]
    copies.append(pltpu.make_async_copy(in_ref.at[:, pl.ds(full * rows, rows // 2), :], tail_ref, sems.at[full]))
    for copy in copies:
        copy.start()
    for copy in copies:
        copy.wait()
    block = 4 * QUAD
    size = block * unit
    span = block * QUAD
    order = selector(size, size, lambda o: (o % span) // QUAD * unit + (o % QUAD) * QUAD + o // span)
    order_tail = selector(
        size, size // 2, lambda o: (o % span) // QUAD * (unit // 2) + (o % QUAD) % 2 * QUAD + o // span
    )
    early = lax.broadcasted_iota(jnp.int32, (size, half), 0) % QUAD < 2
    body = body_ref.reshape(group * rows, full * LANES)
    tail = tail_ref.reshape(group * rows // 2, LANES)
    for i in range(orbs // span):
        clean = dot_nn(order, body[pl.ds(i * size, size), :]).astype(jnp.bfloat16)
        both = dot_nn(order_tail, tail[pl.ds(i * size // 2, size // 2), :])
        last = jnp.where(early, both[:, :half], both[:, half:]).astype(jnp.bfloat16)
        for e in range(QUAD):
            out_ref[e, pl.ds(i * span, span), : full * LANES] = clean[e * span : (e + 1) * span]
            out_ref[e, pl.ds(i * span, span), full * LANES :] = last[e * span : (e + 1) * span]


def unpack(arrived, rows, orbs):
    group = arrived.shape[0]
    full = orbs // LANES
    return pl.pallas_call(
        functools.partial(unpack_kernel, orbs),
        out_shape=jax.ShapeDtypeStruct((QUAD, orbs, orbs), jnp.bfloat16),
        in_specs=[HBM_WHOLE],
        out_specs=VMEM_WHOLE,
        scratch_shapes=[
            pltpu.VMEM((group, rows * QUAD, full * LANES), jnp.bfloat16),
            pltpu.VMEM((group, rows * QUAD // 2, LANES), jnp.bfloat16),
            pltpu.SemaphoreType.DMA((full + 1,)),
        ],
        compiler_params=pltpu.CompilerParams(vmem_limit_bytes=32 * MIB),
        name="unpack",
    )(arrived)


def edge_row(edge, edges, blk_dev):
    return edge * blk_dev // edges


def leaving_kernel(target_ref, rounded_ref, tiles_ref, out_ref, acc_ref):
    blk_dev = rounded_ref.shape[0]
    edges = tiles_ref.shape[0]
    acc_ref[...] = jnp.zeros_like(acc_ref)
    for e in range(edges):

        @pl.when(target_ref[e] >= blk_dev)
        def _(e=e):
            acc_ref[target_ref[e] - blk_dev] += dot_nn(rounded_ref[edge_row(e, edges, blk_dev)], tiles_ref[e])

    out_ref[...] = acc_ref[...].astype(jnp.bfloat16)


def staying_kernel(target_ref, rounded_ref, tiles_ref, after_ref, out_ref):
    blk_dev = rounded_ref.shape[0]
    edges = tiles_ref.shape[0]
    out_ref[...] = jnp.zeros_like(out_ref)
    for e in range(edges):

        @pl.when(target_ref[e] < blk_dev)
        def _(e=e):
            row = edge_row(e, edges, blk_dev)
            out_ref[target_ref[e]] += dot_nn(rounded_ref[row], tiles_ref[e])
            out_ref[row] += dot_nt(rounded_ref[target_ref[e]], tiles_ref[e])


def entering_kernel(target_ref, following_ref, tiles_ref, start_ref, out_ref):
    blk_dev = following_ref.shape[0]
    edges = tiles_ref.shape[0]
    out_ref[...] = start_ref[...]
    for e in range(edges):

        @pl.when(target_ref[e] >= blk_dev)
        def _(e=e):
            out_ref[edge_row(e, edges, blk_dev)] += dot_nt(following_ref[target_ref[e] - blk_dev], tiles_ref[e])


def step_call(kernel, name, dtype, target, panel, tiles, rest=(), scratch=(), rest_specs=()):
    vecs = panel.shape[1]
    return pl.pallas_call(
        kernel,
        out_shape=jax.ShapeDtypeStruct(panel.shape, dtype),
        in_specs=[SMEM_WHOLE, VMEM_WHOLE, VMEM_WHOLE, *rest_specs],
        out_specs=VMEM_WHOLE,
        scratch_shapes=scratch,
        compiler_params=pltpu.CompilerParams(vmem_limit_bytes=16 * MIB),
        cost_estimate=pl.CostEstimate(
            flops=2 * tiles.size * vecs * 4, bytes_accessed=2 * tiles.size, transcendentals=0
        ),
        name=name,
    )(target, panel, tiles, *rest)


def gathered_tiles(edge_tiles, block_total, slots):
    group = lax.axis_size("gx")
    tiles, rows, orbs = edge_tiles.shape
    per_owner = tiles // group
    if per_owner == QUAD and rows % QUAD == 0 and orbs % LANES == LANES // 2 and orbs % (4 * QUAD * QUAD) == 0:
        sent = lax.all_to_all(pack(edge_tiles), "gx", split_axis=0, concat_axis=0, tiled=True)
        return unpack(sent, rows, orbs)
    return lax.all_to_all(edge_tiles, "gx", split_axis=0, concat_axis=1, tiled=True)


def per_device(edge_tiles, trial_panel, col_blocks):
    blk_dev, _, _ = trial_panel.shape
    slots = col_blocks.shape[1]
    block_total = blk_dev * lax.axis_size("gx")
    domain = lax.axis_index("gx")
    own_cols = lax.dynamic_slice_in_dim(col_blocks, domain * blk_dev, blk_dev, 0).reshape(-1)
    target = jnp.mod(own_cols - domain * blk_dev, block_total)
    tiles = gathered_tiles(edge_tiles, block_total, slots)

    def operate(rounded):
        following = passed_along(rounded, "gx", -1)
        send = step_call(
            leaving_kernel,
            "leaving",
            jnp.bfloat16,
            target,
            rounded,
            tiles,
            scratch=[pltpu.VMEM(rounded.shape, jnp.float32)],
        )
        arrive = passed_along(send, "gx", 1)
        home = step_call(
            staying_kernel, "staying", jnp.float32, target, rounded, tiles, (send,), (), (pl.BlockSpec(memory_space=pl.ANY),)
        )
        direct = step_call(entering_kernel, "entering", jnp.float32, target, following, tiles, (home,), (), (VMEM_WHOLE,))
        return direct + arrive.astype(jnp.float32)

    previous = trial_panel
    current = operate(trial_panel.astype(jnp.bfloat16))
    for _ in range(DEGREE - 1):
        following_panel = 2.0 * operate(current.astype(jnp.bfloat16)) - previous
        previous, current = current, following_panel
    return previous, current


def solution(mesh):
    return jax.shard_map(
        per_device,
        mesh=mesh,
        in_specs=(P("member", "gx", None), P(("member", "gx"), None, None), P()),
        out_specs=(P(("member", "gx"), None, None), P(("member", "gx"), None, None)),
        check_vma=False,
    )
```

```python
import functools

import jax
import jax.numpy as jnp
from jax import lax
from jax.experimental import pallas as pl
from jax.experimental.pallas import tpu as pltpu
from jax.sharding import PartitionSpec as P

DEGREE = 4
LANES = 128
QUAD = 4
MIB = 2**20
VMEM_WHOLE = pl.BlockSpec(memory_space=pltpu.VMEM)
HBM_WHOLE = pl.BlockSpec(memory_space=pltpu.HBM)
SMEM_WHOLE = pl.BlockSpec(memory_space=pltpu.SMEM)


def passed_along(value, axis, steps):
    count = lax.axis_size(axis)
    pairs = [(source, (source + steps) % count) for source in range(count)]
    return lax.ppermute(value, axis, pairs)


def dot_nn(a, b):
    return lax.dot_general(a, b, (((1,), (0,)), ((), ())), preferred_element_type=jnp.float32)


def dot_nt(a, b):
    return lax.dot_general(a, b, (((1,), (1,)), ((), ())), preferred_element_type=jnp.float32)


def selector(rows, columns, source_of_row):
    row = lax.broadcasted_iota(jnp.int32, (rows, columns), 0)
    column = lax.broadcasted_iota(jnp.int32, (rows, columns), 1)
    return (column == source_of_row(row)).astype(jnp.bfloat16)


def pack_kernel(batch, x_ref, out_ref, x_buf, out_buf, tail_buf, in_sems, out_sems):
    rows, tiles, orbs = x_ref.shape
    group = tiles // QUAD
    unit = QUAD * QUAD
    steps = rows // QUAD
    full = orbs // LANES
    half = LANES // 2
    length = steps * unit
    arrivals = []
    for j in range(steps):
        part = pl.ds(j * QUAD, QUAD)
        arrivals.append(pltpu.make_async_copy(x_ref.at[part], x_buf.at[part], in_sems.at[j]))
        arrivals[-1].start()
    order = selector(QUAD * tiles, QUAD * tiles, lambda o: ((o % unit) // QUAD) * tiles + (o // unit) * QUAD + o % QUAD)
    leaving = []

    def leave(first, count):
        part = pl.ds(first, count)
        copy = pltpu.make_async_copy(out_buf.at[:, part, :], out_ref.at[:, part, :], out_sems.at[len(leaving)])
        copy.start()
        leaving.append(copy)

    begun = 0
    for j in range(steps):
        arrivals[j].wait()
        data = x_buf[j * QUAD : (j + 1) * QUAD].reshape(QUAD * tiles, orbs)
        for left in range(0, full * LANES, 2 * LANES):
            width = min(2 * LANES, full * LANES - left)
            part = dot_nn(order, data[:, left : left + width]).astype(jnp.bfloat16)
            for k in range(0, width, LANES):
                first = (left + k) // LANES * length + j * unit
                out_buf[:, first : first + unit, :] = part[:, k : k + LANES].reshape(group, unit, LANES)
        last = dot_nn(order, data[:, full * LANES :]).reshape(group, unit, half)
        both = jnp.concatenate([last[:, : unit // 2], last[:, unit // 2 :]], axis=2)
        tail_buf[:, j * unit // 2 : (j + 1) * unit // 2, :] = both
        if (j + 1) % batch == 0 or j == steps - 1:
            for k in range(full):
                leave(k * length + begun * unit, (j + 1 - begun) * unit)
            begun = j + 1
    out_buf[:, full * length :, :] = tail_buf[...].astype(jnp.bfloat16)
    leave(full * length, length // 2)
    for copy in leaving:
        copy.wait()


def pack(edge_tiles):
    tiles, rows, orbs = edge_tiles.shape
    group = tiles // QUAD
    turned = jnp.transpose(edge_tiles, (1, 0, 2))
    flat = rows * QUAD * orbs // LANES
    steps = rows // QUAD
    batch = 4
    copies = -(-steps // batch) * (orbs // LANES) + 1
    return pl.pallas_call(
        functools.partial(pack_kernel, batch),
        out_shape=jax.ShapeDtypeStruct((group, flat, LANES), jnp.bfloat16),
        in_specs=[HBM_WHOLE],
        out_specs=HBM_WHOLE,
        scratch_shapes=[
            pltpu.VMEM((rows, tiles, orbs), jnp.bfloat16),
            pltpu.VMEM((group, flat, LANES), jnp.bfloat16),
            pltpu.VMEM((group, rows * QUAD // 2, LANES), jnp.float32),
            pltpu.SemaphoreType.DMA((steps,)),
            pltpu.SemaphoreType.DMA((copies,)),
        ],
        compiler_params=pltpu.CompilerParams(vmem_limit_bytes=58 * MIB),
        name="pack",
    )(turned)


def unpack_kernel(orbs, in_ref, out_ref, body_ref, tail_ref, sems):
    group, rows, _ = body_ref.shape
    full = orbs // LANES
    half = LANES // 2
    unit = QUAD * QUAD
    stages = sems.shape[0]
    sources = group // stages
    arrivals = []
    for g in range(stages):
        part = pl.ds(g * sources, sources)
        copies = [
            pltpu.make_async_copy(
                in_ref.at[part, pl.ds(j * rows, rows), :], body_ref.at[part, :, pl.ds(j * LANES, LANES)], sems.at[g, j]
            )
            for j in range(full)
        ]
        copies.append(
            pltpu.make_async_copy(in_ref.at[part, pl.ds(full * rows, rows // 2), :], tail_ref.at[part], sems.at[g, full])
        )
        for copy in copies:
            copy.start()
        arrivals.append(copies)
    here = 0
    block = 4 * QUAD
    size = block * unit
    span = block * QUAD
    order = selector(size, size, lambda o: (o % span) // QUAD * unit + (o % QUAD) * QUAD + o // span)
    order_tail = selector(
        size, size // 2, lambda o: (o % span) // QUAD * (unit // 2) + (o % QUAD) % 2 * QUAD + o // span
    )
    early = lax.broadcasted_iota(jnp.int32, (size, half), 0) % QUAD < 2
    body = body_ref.reshape(group * rows, full * LANES)
    tail = tail_ref.reshape(group * rows // 2, LANES)
    for i in range(orbs // span):
        while here * sources * rows < (i + 1) * size:
            for copy in arrivals[here]:
                copy.wait()
            here += 1
        clean = dot_nn(order, body[pl.ds(i * size, size), :]).astype(jnp.bfloat16)
        both = dot_nn(order_tail, tail[pl.ds(i * size // 2, size // 2), :])
        last = jnp.where(early, both[:, :half], both[:, half:]).astype(jnp.bfloat16)
        for e in range(QUAD):
            out_ref[e, pl.ds(i * span, span), : full * LANES] = clean[e * span : (e + 1) * span]
            out_ref[e, pl.ds(i * span, span), full * LANES :] = last[e * span : (e + 1) * span]


def unpack(arrived, rows, orbs):
    group = arrived.shape[0]
    full = orbs // LANES
    return pl.pallas_call(
        functools.partial(unpack_kernel, orbs),
        out_shape=jax.ShapeDtypeStruct((QUAD, orbs, orbs), jnp.bfloat16),
        in_specs=[HBM_WHOLE],
        out_specs=VMEM_WHOLE,
        scratch_shapes=[
            pltpu.VMEM((group, rows * QUAD, full * LANES), jnp.bfloat16),
            pltpu.VMEM((group, rows * QUAD // 2, LANES), jnp.bfloat16),
            pltpu.SemaphoreType.DMA((4 if group % 4 == 0 else 1, full + 1)),
        ],
        compiler_params=pltpu.CompilerParams(vmem_limit_bytes=32 * MIB),
        name="unpack",
    )(arrived)


def turned_kernel(target_ref, rounded_ref, tiles_ref, own_ref, send_ref, acc_ref):
    blk_dev = rounded_ref.shape[0]
    edges = tiles_ref.shape[0]
    acc_ref[...] = jnp.zeros_like(acc_ref)
    for e in range(edges):
        acc_ref[target_ref[e]] += dot_nn(rounded_ref[e * blk_dev // edges], tiles_ref[e])
    own_ref[...] = acc_ref[:blk_dev]
    send_ref[...] = acc_ref[blk_dev:].astype(jnp.bfloat16)


def turned_terms(target, rounded, tiles):
    blk_dev, vecs, orbs = rounded.shape
    return pl.pallas_call(
        turned_kernel,
        out_shape=(
            jax.ShapeDtypeStruct(rounded.shape, jnp.float32),
            jax.ShapeDtypeStruct(rounded.shape, jnp.bfloat16),
        ),
        in_specs=[SMEM_WHOLE, VMEM_WHOLE, VMEM_WHOLE],
        out_specs=(VMEM_WHOLE, VMEM_WHOLE),
        scratch_shapes=[pltpu.VMEM((2 * blk_dev, vecs, orbs), jnp.float32)],
        compiler_params=pltpu.CompilerParams(vmem_limit_bytes=16 * MIB),
        cost_estimate=pl.CostEstimate(
            flops=2 * tiles.size * vecs * 4, bytes_accessed=2 * tiles.size, transcendentals=0
        ),
        name="turned",
    )(target, rounded, tiles)


def direct_kernel(target_ref, rounded_ref, following_ref, tiles_ref, own_ref, out_ref, picked_ref):
    blk_dev = rounded_ref.shape[0]
    edges = tiles_ref.shape[0]
    slots = edges // blk_dev
    picked_ref[:blk_dev] = rounded_ref[...]
    picked_ref[blk_dev:] = following_ref[...]
    for b in range(blk_dev):
        total = own_ref[b]
        for e in range(b * slots, (b + 1) * slots):
            total += dot_nn(picked_ref[target_ref[e]], tiles_ref[e])
        out_ref[b] = total


def direct_terms(target, rounded, following, tiles, own):
    blk_dev, vecs, orbs = rounded.shape
    return pl.pallas_call(
        direct_kernel,
        out_shape=jax.ShapeDtypeStruct(rounded.shape, jnp.float32),
        in_specs=[SMEM_WHOLE] + [VMEM_WHOLE] * 4,
        out_specs=VMEM_WHOLE,
        scratch_shapes=[pltpu.VMEM((2 * blk_dev, vecs, orbs), jnp.bfloat16)],
        compiler_params=pltpu.CompilerParams(vmem_limit_bytes=16 * MIB),
        cost_estimate=pl.CostEstimate(
            flops=2 * tiles.size * vecs * 4, bytes_accessed=2 * tiles.size, transcendentals=0
        ),
        name="direct",
    )(target, rounded, following, tiles, own)


def mirror_kernel(tiles_ref, after_ref, out_ref):
    for e in range(tiles_ref.shape[0]):
        out_ref[e] = tiles_ref[e].T


def mirrored(tiles, after):
    return pl.pallas_call(
        mirror_kernel,
        out_shape=jax.ShapeDtypeStruct(tiles.shape, tiles.dtype),
        in_specs=[VMEM_WHOLE, pl.BlockSpec(memory_space=pl.ANY)],
        out_specs=VMEM_WHOLE,
        compiler_params=pltpu.CompilerParams(vmem_limit_bytes=16 * MIB),
        cost_estimate=pl.CostEstimate(flops=tiles.size * 400, bytes_accessed=4 * tiles.size, transcendentals=0),
        name="mirror",
    )(tiles, after)


def update_kernel(direct_ref, arrive_ref, previous_ref, panel_ref, rounded_ref):
    panel = 2.0 * (direct_ref[...] + arrive_ref[...].astype(jnp.float32)) - previous_ref[...]
    panel_ref[...] = panel
    rounded_ref[...] = panel.astype(jnp.bfloat16)


def updated(direct, arrive, previous):
    return pl.pallas_call(
        update_kernel,
        out_shape=(
            jax.ShapeDtypeStruct(direct.shape, jnp.float32),
            jax.ShapeDtypeStruct(direct.shape, jnp.bfloat16),
        ),
        in_specs=[VMEM_WHOLE] * 3,
        out_specs=(VMEM_WHOLE, VMEM_WHOLE),
        compiler_params=pltpu.CompilerParams(vmem_limit_bytes=16 * MIB),
        name="update",
    )(direct, arrive, previous)


def gathered_tiles(edge_tiles, block_total, slots):
    group = lax.axis_size("gx")
    tiles, rows, orbs = edge_tiles.shape
    per_owner = tiles // group
    if per_owner == QUAD and rows % QUAD == 0 and orbs % LANES == LANES // 2 and orbs % (4 * QUAD * QUAD) == 0:
        sent = lax.all_to_all(pack(edge_tiles), "gx", split_axis=0, concat_axis=0, tiled=True)
        return unpack(sent, rows, orbs)
    return lax.all_to_all(edge_tiles, "gx", split_axis=0, concat_axis=1, tiled=True)


def per_device(edge_tiles, trial_panel, col_blocks):
    blk_dev, _, _ = trial_panel.shape
    slots = col_blocks.shape[1]
    block_total = blk_dev * lax.axis_size("gx")
    domain = lax.axis_index("gx")
    own_cols = lax.dynamic_slice_in_dim(col_blocks, domain * blk_dev, blk_dev, 0).reshape(-1)
    target = jnp.mod(own_cols - domain * blk_dev, block_total)
    tiles = gathered_tiles(edge_tiles, block_total, slots)
    mirror = None
    previous, current = None, trial_panel
    rounded = trial_panel.astype(jnp.bfloat16)
    for k in range(DEGREE):
        following = passed_along(rounded, "gx", -1)
        own, send = turned_terms(target, rounded, tiles)
        arrive = passed_along(send, "gx", 1)
        if k == 0:
            mirror = mirrored(tiles, send)
        direct = direct_terms(target, rounded, following, mirror, own)
        if k == 0:
            total = direct + arrive.astype(jnp.float32)
            rounded = total.astype(jnp.bfloat16)
        elif k < DEGREE - 1:
            total, rounded = updated(direct, arrive, previous)
        else:
            total = 2.0 * (direct + arrive.astype(jnp.float32)) - previous
        previous, current = current, total
    return previous, current


def solution(mesh):
    return jax.shard_map(
        per_device,
        mesh=mesh,
        in_specs=(P("member", "gx", None), P(("member", "gx"), None, None), P()),
        out_specs=(P(("member", "gx"), None, None), P(("member", "gx"), None, None)),
        check_vma=False,
    )
```

```python
import functools

import jax
import jax.numpy as jnp
from jax import lax
from jax.experimental import pallas as pl
from jax.experimental.pallas import tpu as pltpu
from jax.sharding import PartitionSpec as P

DEGREE = 4
LANES = 128
QUAD = 4
MIB = 2**20
VMEM_WHOLE = pl.BlockSpec(memory_space=pltpu.VMEM)
HBM_WHOLE = pl.BlockSpec(memory_space=pltpu.HBM)
SMEM_WHOLE = pl.BlockSpec(memory_space=pltpu.SMEM)


def passed_along(value, axis, steps):
    count = lax.axis_size(axis)
    pairs = [(source, (source + steps) % count) for source in range(count)]
    return lax.ppermute(value, axis, pairs)


def dot_nn(a, b):
    return lax.dot_general(a, b, (((1,), (0,)), ((), ())), preferred_element_type=jnp.float32)


def dot_nt(a, b):
    return lax.dot_general(a, b, (((1,), (1,)), ((), ())), preferred_element_type=jnp.float32)


def selector(rows, columns, source_of_row):
    row = lax.broadcasted_iota(jnp.int32, (rows, columns), 0)
    column = lax.broadcasted_iota(jnp.int32, (rows, columns), 1)
    return (column == source_of_row(row)).astype(jnp.bfloat16)


def pack_kernel(left, bounds, x_ref, out_ref, x_buf, out_buf, tail_buf, in_sems, out_sems):
    rows, tiles, width = x_buf.shape
    group = tiles // QUAD
    unit = QUAD * QUAD
    steps = rows // QUAD
    full = width // LANES
    half = LANES // 2
    has_tail = width % LANES > 0
    length = steps * unit
    arrivals = []
    for stage, (start, stop) in enumerate(zip(bounds[:-1], bounds[1:])):
        part = pl.ds(start * QUAD, (stop - start) * QUAD)
        arrivals.append(
            pltpu.make_async_copy(x_ref.at[part, :, pl.ds(left, width)], x_buf.at[part], in_sems.at[stage])
        )
        arrivals[-1].start()
    order = selector(QUAD * tiles, QUAD * tiles, lambda o: ((o % unit) // QUAD) * tiles + (o // unit) * QUAD + o % QUAD)
    leaving = []

    def leave(first, count):
        part = pl.ds(first, count)
        copy = pltpu.make_async_copy(out_buf.at[:, part, :], out_ref.at[:, part, :], out_sems.at[len(leaving)])
        copy.start()
        leaving.append(copy)

    begun = 0
    for j in range(steps):
        if j in bounds:
            arrivals[bounds.index(j)].wait()
        data = x_buf[j * QUAD : (j + 1) * QUAD].reshape(QUAD * tiles, width)
        for at in range(0, full * LANES, 2 * LANES):
            wide = min(2 * LANES, full * LANES - at)
            part = dot_nn(order, data[:, at : at + wide]).astype(jnp.bfloat16)
            for k in range(0, wide, LANES):
                first = (at + k) // LANES * length + j * unit
                out_buf[:, first : first + unit, :] = part[:, k : k + LANES].reshape(group, unit, LANES)
        if has_tail:
            last = dot_nn(order, data[:, full * LANES :]).reshape(group, unit, half)
            both = jnp.concatenate([last[:, : unit // 2], last[:, unit // 2 :]], axis=2)
            tail_buf[:, j * unit // 2 : (j + 1) * unit // 2, :] = both
        if j + 1 in bounds:
            for k in range(full):
                leave(k * length + begun * unit, (j + 1 - begun) * unit)
            begun = j + 1
    if has_tail:
        out_buf[:, full * length :, :] = tail_buf[...].astype(jnp.bfloat16)
        leave(full * length, length // 2)
    for copy in leaving:
        copy.wait()


def pack(edge_tiles, left, width):
    tiles, rows, _ = edge_tiles.shape
    group = tiles // QUAD
    turned = jnp.transpose(edge_tiles, (1, 0, 2))
    flat = rows * QUAD * width // LANES
    steps = rows // QUAD
    bounds = tuple(sorted({0, -(-3 * steps // 8), -(-6 * steps // 8), steps}))
    stages = len(bounds) - 1
    return pl.pallas_call(
        functools.partial(pack_kernel, left, bounds),
        out_shape=jax.ShapeDtypeStruct((group, flat, LANES), jnp.bfloat16),
        in_specs=[HBM_WHOLE],
        out_specs=HBM_WHOLE,
        scratch_shapes=[
            pltpu.VMEM((rows, tiles, width), jnp.bfloat16),
            pltpu.VMEM((group, flat, LANES), jnp.bfloat16),
            pltpu.VMEM((group, rows * QUAD // 2, LANES), jnp.float32),
            pltpu.SemaphoreType.DMA((stages,)),
            pltpu.SemaphoreType.DMA((stages * (width // LANES) + 1,)),
        ],
        compiler_params=pltpu.CompilerParams(vmem_limit_bytes=58 * MIB),
        cost_estimate=pl.CostEstimate(
            flops=2 * rows * tiles * width * 4 * tiles, bytes_accessed=4 * rows * tiles * width, transcendentals=0
        ),
        name="pack",
    )(turned)


def unpack_kernel(rows, bounds, from_ref, out_ref, in_ref, sems):
    _, orbs, width = out_ref.shape
    full = width // LANES
    half = LANES // 2
    unit = QUAD * QUAD
    block = 4 * QUAD
    size = block * unit
    span = block * QUAD
    order = selector(size, size, lambda o: (o % span) // QUAD * unit + (o % QUAD) * QUAD + o // span)
    order_tail = selector(
        size, size // 2, lambda o: (o % span) // QUAD * (unit // 2) + (o % QUAD) % 2 * QUAD + o // span
    )
    early = lax.broadcasted_iota(jnp.int32, (size, half), 0) % QUAD < 2
    arrivals = []
    for stage, (start, stop) in enumerate(zip(bounds[:-1], bounds[1:])):
        part = pl.ds(start, stop - start)
        arrivals.append(pltpu.make_async_copy(from_ref.at[part], in_ref.at[part], sems.at[stage]))
        arrivals[-1].start()
    here = 0

    def lane_block(j, start, stop, scale):
        held = rows // scale
        pieces = []
        while start < stop:
            g, at = divmod(start, held)
            count = min(stop - start, held - at)
            pieces.append(in_ref[g, j * rows + at : j * rows + at + count, :])
            start += count
        return pieces[0] if len(pieces) == 1 else jnp.concatenate(pieces, axis=0)

    for i in range(orbs // span):
        while bounds[here] * rows < (i + 1) * size:
            arrivals[here].wait()
            here += 1
        for at in range(0, full, 2):
            wide = range(at, min(at + 2, full))
            data = jnp.concatenate([lane_block(j, i * size, (i + 1) * size, 1) for j in wide], axis=1)
            clean = dot_nn(order, data).astype(jnp.bfloat16)
            for e in range(QUAD):
                place = slice(at * LANES, (at + len(wide)) * LANES)
                out_ref[e, pl.ds(i * span, span), place] = clean[e * span : (e + 1) * span]
        if width % LANES:
            both = dot_nn(order_tail, lane_block(full, i * size // 2, (i + 1) * size // 2, 2))
            last = jnp.where(early, both[:, :half], both[:, half:]).astype(jnp.bfloat16)
            for e in range(QUAD):
                out_ref[e, pl.ds(i * span, span), full * LANES :] = last[e * span : (e + 1) * span]


def unpack(arrived, rows, orbs, width):
    group = arrived.shape[0]
    bounds = tuple(sorted({0, group // 2, group}))
    return pl.pallas_call(
        functools.partial(unpack_kernel, rows * QUAD, bounds),
        out_shape=jax.ShapeDtypeStruct((QUAD, orbs, width), jnp.bfloat16),
        in_specs=[HBM_WHOLE],
        out_specs=VMEM_WHOLE,
        scratch_shapes=[pltpu.VMEM(arrived.shape, arrived.dtype), pltpu.SemaphoreType.DMA((len(bounds) - 1,))],
        compiler_params=pltpu.CompilerParams(vmem_limit_bytes=20 * MIB),
        cost_estimate=pl.CostEstimate(
            flops=2 * QUAD * orbs * width * 256, bytes_accessed=4 * QUAD * orbs * width, transcendentals=0
        ),
        name="unpack",
    )(arrived)


def product_cost(parts, vecs):
    size = sum(part.size for part in parts)
    return pl.CostEstimate(flops=2 * size * vecs * 4, bytes_accessed=2 * size, transcendentals=0)


def turned_kernel(count, target_ref, rounded_ref, *refs):
    parts, early, (own_ref, send_ref, acc_ref) = refs[:count], refs[count:-3], refs[-3:]
    blk_dev = rounded_ref.shape[0]
    at = 0
    if early:
        at = early[0].shape[2]
        own_ref[:, :, :at] = early[0][...]
        send_ref[:, :, :at] = early[1][...]
    left = at
    acc_ref[...] = jnp.zeros_like(acc_ref)
    for part in parts:
        edges, _, width = part.shape
        for e in range(edges):
            acc_ref[target_ref[e], :, left : left + width] += dot_nn(rounded_ref[e * blk_dev // edges], part[e])
        left += width
    own_ref[:, :, at:] = acc_ref[:blk_dev, :, at:]
    send_ref[:, :, at:] = acc_ref[blk_dev:, :, at:].astype(jnp.bfloat16)


def turned_terms(target, rounded, parts, early=()):
    blk_dev, vecs, _ = rounded.shape
    shape = (blk_dev, vecs, sum(part.shape[2] for part in [*early[:1], *parts]))
    return pl.pallas_call(
        functools.partial(turned_kernel, len(parts)),
        out_shape=(jax.ShapeDtypeStruct(shape, jnp.float32), jax.ShapeDtypeStruct(shape, jnp.bfloat16)),
        in_specs=[SMEM_WHOLE] + [VMEM_WHOLE] * (1 + len(parts) + len(early)),
        out_specs=(VMEM_WHOLE, VMEM_WHOLE),
        scratch_shapes=[pltpu.VMEM((2 * blk_dev, *shape[1:]), jnp.float32)],
        compiler_params=pltpu.CompilerParams(vmem_limit_bytes=16 * MIB),
        cost_estimate=product_cost(parts, vecs),
        name="turned",
    )(target, rounded, *parts, *early)


def direct_kernel(target_ref, rounded_ref, following_ref, own_ref, *refs):
    mirrors, (out_ref, picked_ref) = refs[:-2], refs[-2:]
    blk_dev = rounded_ref.shape[0]
    edges = mirrors[0].shape[0]
    slots = edges // blk_dev
    picked_ref[:blk_dev] = rounded_ref[...]
    picked_ref[blk_dev:] = following_ref[...]
    for b in range(blk_dev):
        total = own_ref[b]
        for e in range(b * slots, (b + 1) * slots):
            left = 0
            for mirror in mirrors:
                width = mirror.shape[1]
                total += dot_nn(picked_ref[target_ref[e], :, left : left + width], mirror[e])
                left += width
        out_ref[b] = total


def direct_terms(target, rounded, following, own, mirrors):
    blk_dev, vecs, orbs = rounded.shape
    return pl.pallas_call(
        direct_kernel,
        out_shape=jax.ShapeDtypeStruct(rounded.shape, jnp.float32),
        in_specs=[SMEM_WHOLE] + [VMEM_WHOLE] * (3 + len(mirrors)),
        out_specs=VMEM_WHOLE,
        scratch_shapes=[pltpu.VMEM((2 * blk_dev, vecs, orbs), jnp.bfloat16)],
        compiler_params=pltpu.CompilerParams(vmem_limit_bytes=16 * MIB),
        cost_estimate=product_cost(mirrors, vecs),
        name="direct",
    )(target, rounded, following, own, *mirrors)


def mirror_kernel(tiles_ref, after_ref, out_ref):
    for e in range(tiles_ref.shape[0]):
        out_ref[e] = tiles_ref[e].T


def mirrored(tiles, after):
    edges, rows, width = tiles.shape
    return pl.pallas_call(
        mirror_kernel,
        out_shape=jax.ShapeDtypeStruct((edges, width, rows), tiles.dtype),
        in_specs=[VMEM_WHOLE, pl.BlockSpec(memory_space=pl.ANY)],
        out_specs=VMEM_WHOLE,
        compiler_params=pltpu.CompilerParams(vmem_limit_bytes=16 * MIB),
        cost_estimate=pl.CostEstimate(flops=tiles.size * 400, bytes_accessed=4 * tiles.size, transcendentals=0),
        name="mirror",
    )(tiles, after)


def rounded_kernel(direct_ref, arrive_ref, previous_ref, rounded_ref):
    panel = 2.0 * (direct_ref[...] + arrive_ref[...].astype(jnp.float32)) - previous_ref[...]
    rounded_ref[...] = panel.astype(jnp.bfloat16)


def rounded_update(direct, arrive, previous):
    return pl.pallas_call(
        rounded_kernel,
        out_shape=jax.ShapeDtypeStruct(direct.shape, jnp.bfloat16),
        in_specs=[VMEM_WHOLE] * 3,
        out_specs=VMEM_WHOLE,
        compiler_params=pltpu.CompilerParams(vmem_limit_bytes=16 * MIB),
        name="rounded",
    )(direct, arrive, previous)


def exchanged(tiles):
    return lax.all_to_all(tiles, "gx", split_axis=0, concat_axis=0, tiled=True)


def per_device(edge_tiles, trial_panel, col_blocks):
    blk_dev, _, orbs = trial_panel.shape
    tiles, rows, _ = edge_tiles.shape
    group = lax.axis_size("gx")
    block_total = blk_dev * group
    domain = lax.axis_index("gx")
    own_cols = lax.dynamic_slice_in_dim(col_blocks, domain * blk_dev, blk_dev, 0).reshape(-1)
    target = jnp.mod(own_cols - domain * blk_dev, block_total)
    rounded = trial_panel.astype(jnp.bfloat16)
    fits = tiles // group == QUAD and rows % QUAD == 0
    if fits and orbs % LANES == LANES // 2 and orbs % (4 * QUAD * QUAD) == 0:
        cuts = [(0, orbs)]
        parts = [unpack(exchanged(pack(edge_tiles, *cut)), rows, orbs, cut[1]) for cut in cuts]
    else:
        parts = [lax.all_to_all(edge_tiles, "gx", split_axis=0, concat_axis=1, tiled=True)]
    early = turned_terms(target, rounded, parts[:1]) if len(parts) > 1 else ()
    mirrors = [mirrored(part, early[1]) for part in parts[:-1]]

    previous, current = None, trial_panel
    for k in range(DEGREE):
        following = passed_along(rounded, "gx", -1)
        if k == 0:
            own, send = turned_terms(target, rounded, parts[len(parts) - 1 :], early)
            mirrors.append(mirrored(parts[-1], send))
        else:
            own, send = turned_terms(target, rounded, parts)
        arrive = passed_along(send, "gx", 1)
        direct = direct_terms(target, rounded, following, own, mirrors)
        if k == 0:
            total = direct + arrive.astype(jnp.float32)
            rounded = total.astype(jnp.bfloat16)
        else:
            if k == DEGREE - 2:
                rounded = rounded_update(direct, arrive, previous)
                direct, arrive, previous, rounded = lax.optimization_barrier((direct, arrive, previous, rounded))
            total = 2.0 * (direct + arrive.astype(jnp.float32)) - previous
            if k < DEGREE - 2:
                rounded = total.astype(jnp.bfloat16)
        previous, current = current, total
    return previous, current


def solution(mesh):
    return jax.shard_map(
        per_device,
        mesh=mesh,
        in_specs=(P("member", "gx", None), P(("member", "gx"), None, None), P()),
        out_specs=(P(("member", "gx"), None, None), P(("member", "gx"), None, None)),
        check_vma=False,
    )
```

```python
import functools

import jax
import jax.numpy as jnp
from jax import lax
from jax.experimental import pallas as pl
from jax.experimental.pallas import tpu as pltpu
from jax.sharding import PartitionSpec as P

DEGREE = 4
LANES = 128
QUAD = 4
MIB = 2**20
VMEM_WHOLE = pl.BlockSpec(memory_space=pltpu.VMEM)
HBM_WHOLE = pl.BlockSpec(memory_space=pltpu.HBM)
SUBLANES = 8


def passed_along(value, axis, steps):
    count = lax.axis_size(axis)
    pairs = [(source, (source + steps) % count) for source in range(count)]
    return lax.ppermute(value, axis, pairs)


def dot_nn(a, b):
    return lax.dot_general(a, b, (((1,), (0,)), ((), ())), preferred_element_type=jnp.float32)


def dot_nt(a, b):
    return lax.dot_general(a, b, (((1,), (1,)), ((), ())), preferred_element_type=jnp.float32)


def selector(rows, columns, source_of_row):
    row = lax.broadcasted_iota(jnp.int32, (rows, columns), 0)
    column = lax.broadcasted_iota(jnp.int32, (rows, columns), 1)
    return (column == source_of_row(row)).astype(jnp.bfloat16)


def pack_kernel(left, bounds, x_ref, out_ref, x_buf, out_buf, tail_buf, in_sems, out_sems):
    rows, tiles, width = x_buf.shape
    group = tiles // QUAD
    unit = QUAD * QUAD
    steps = rows // QUAD
    full = width // LANES
    half = LANES // 2
    has_tail = width % LANES > 0
    length = steps * unit
    arrivals = []
    for stage, (start, stop) in enumerate(zip(bounds[:-1], bounds[1:])):
        part = pl.ds(start * QUAD, (stop - start) * QUAD)
        arrivals.append(
            pltpu.make_async_copy(x_ref.at[part, :, pl.ds(left, width)], x_buf.at[part], in_sems.at[stage])
        )
        arrivals[-1].start()
    order = selector(QUAD * tiles, QUAD * tiles, lambda o: ((o % unit) // QUAD) * tiles + (o // unit) * QUAD + o % QUAD)
    leaving = []

    def leave(first, count):
        part = pl.ds(first, count)
        copy = pltpu.make_async_copy(out_buf.at[:, part, :], out_ref.at[:, part, :], out_sems.at[len(leaving)])
        copy.start()
        leaving.append(copy)

    begun = 0
    for j in range(steps):
        if j in bounds:
            arrivals[bounds.index(j)].wait()
        data = x_buf[j * QUAD : (j + 1) * QUAD].reshape(QUAD * tiles, width)
        for at in range(0, full * LANES, 2 * LANES):
            wide = min(2 * LANES, full * LANES - at)
            part = dot_nn(order, data[:, at : at + wide]).astype(jnp.bfloat16)
            for k in range(0, wide, LANES):
                first = (at + k) // LANES * length + j * unit
                out_buf[:, first : first + unit, :] = part[:, k : k + LANES].reshape(group, unit, LANES)
        if has_tail:
            last = dot_nn(order, data[:, full * LANES :]).reshape(group, unit, half)
            both = jnp.concatenate([last[:, : unit // 2], last[:, unit // 2 :]], axis=2)
            tail_buf[:, j * unit // 2 : (j + 1) * unit // 2, :] = both
        if j + 1 in bounds:
            for k in range(full):
                leave(k * length + begun * unit, (j + 1 - begun) * unit)
            begun = j + 1
    if has_tail:
        out_buf[:, full * length :, :] = tail_buf[...].astype(jnp.bfloat16)
        leave(full * length, length // 2)
    for copy in leaving:
        copy.wait()


def pack(edge_tiles, left, width):
    tiles, rows, _ = edge_tiles.shape
    group = tiles // QUAD
    turned = jnp.transpose(edge_tiles, (1, 0, 2))
    flat = rows * QUAD * width // LANES
    steps = rows // QUAD
    bounds = tuple(sorted({0, -(-3 * steps // 8), -(-6 * steps // 8), steps}))
    stages = len(bounds) - 1
    return pl.pallas_call(
        functools.partial(pack_kernel, left, bounds),
        out_shape=jax.ShapeDtypeStruct((group, flat, LANES), jnp.bfloat16),
        in_specs=[HBM_WHOLE],
        out_specs=HBM_WHOLE,
        scratch_shapes=[
            pltpu.VMEM((rows, tiles, width), jnp.bfloat16),
            pltpu.VMEM((group, flat, LANES), jnp.bfloat16),
            pltpu.VMEM((group, rows * QUAD // 2, LANES), jnp.float32),
            pltpu.SemaphoreType.DMA((stages,)),
            pltpu.SemaphoreType.DMA((stages * (width // LANES) + 1,)),
        ],
        compiler_params=pltpu.CompilerParams(vmem_limit_bytes=58 * MIB),
        cost_estimate=pl.CostEstimate(
            flops=2 * rows * tiles * width * 4 * tiles, bytes_accessed=4 * rows * tiles * width, transcendentals=0
        ),
        name="pack",
    )(turned)


def unpack_kernel(rows, bounds, from_ref, out_ref, in_ref, sems):
    _, orbs, width = out_ref.shape
    full = width // LANES
    half = LANES // 2
    unit = QUAD * QUAD
    block = 4 * QUAD
    size = block * unit
    span = block * QUAD
    order = selector(size, size, lambda o: (o % span) // QUAD * unit + (o % QUAD) * QUAD + o // span)
    order_tail = selector(
        size, size // 2, lambda o: (o % span) // QUAD * (unit // 2) + (o % QUAD) % 2 * QUAD + o // span
    )
    early = lax.broadcasted_iota(jnp.int32, (size, half), 0) % QUAD < 2
    arrivals = []
    for stage, (start, stop) in enumerate(zip(bounds[:-1], bounds[1:])):
        part = pl.ds(start, stop - start)
        arrivals.append(pltpu.make_async_copy(from_ref.at[part], in_ref.at[part], sems.at[stage]))
        arrivals[-1].start()
    here = 0

    def lane_block(j, start, stop, scale):
        held = rows // scale
        pieces = []
        while start < stop:
            g, at = divmod(start, held)
            count = min(stop - start, held - at)
            pieces.append(in_ref[g, j * rows + at : j * rows + at + count, :])
            start += count
        return pieces[0] if len(pieces) == 1 else jnp.concatenate(pieces, axis=0)

    for i in range(orbs // span):
        while bounds[here] * rows < (i + 1) * size:
            arrivals[here].wait()
            here += 1
        for at in range(0, full, 2):
            wide = range(at, min(at + 2, full))
            data = jnp.concatenate([lane_block(j, i * size, (i + 1) * size, 1) for j in wide], axis=1)
            clean = dot_nn(order, data).astype(jnp.bfloat16)
            for e in range(QUAD):
                place = slice(at * LANES, (at + len(wide)) * LANES)
                out_ref[e, pl.ds(i * span, span), place] = clean[e * span : (e + 1) * span]
        if width % LANES:
            both = dot_nn(order_tail, lane_block(full, i * size // 2, (i + 1) * size // 2, 2))
            last = jnp.where(early, both[:, :half], both[:, half:]).astype(jnp.bfloat16)
            for e in range(QUAD):
                out_ref[e, pl.ds(i * span, span), full * LANES :] = last[e * span : (e + 1) * span]


def unpack(arrived, rows, orbs, width):
    group = arrived.shape[0]
    bounds = tuple(sorted({0, group // 2, group}))
    return pl.pallas_call(
        functools.partial(unpack_kernel, rows * QUAD, bounds),
        out_shape=jax.ShapeDtypeStruct((QUAD, orbs, width), jnp.bfloat16),
        in_specs=[HBM_WHOLE],
        out_specs=VMEM_WHOLE,
        scratch_shapes=[pltpu.VMEM(arrived.shape, arrived.dtype), pltpu.SemaphoreType.DMA((len(bounds) - 1,))],
        compiler_params=pltpu.CompilerParams(vmem_limit_bytes=20 * MIB),
        cost_estimate=pl.CostEstimate(
            flops=2 * QUAD * orbs * width * 256, bytes_accessed=4 * QUAD * orbs * width, transcendentals=0
        ),
        name="unpack",
    )(arrived)


def product_cost(parts, vecs):
    size = sum(part.size for part in parts)
    return pl.CostEstimate(flops=2 * size * vecs * 4, bytes_accessed=2 * size, transcendentals=0)


def turned_kernel(count, target_ref, rounded_ref, *refs):
    parts, early, (own_ref, send_ref, acc_ref) = refs[:count], refs[count:-3], refs[-3:]
    targets = [target_ref[...][e, 0] for e in range(parts[0].shape[0])]
    blk_dev = rounded_ref.shape[0]
    at = 0
    if early:
        at = early[0].shape[2]
        own_ref[:, :, :at] = early[0][...]
        send_ref[:, :, :at] = early[1][...]
    left = at
    acc_ref[...] = jnp.zeros_like(acc_ref)
    for part in parts:
        edges, _, width = part.shape
        for e in range(edges):
            acc_ref[targets[e], :, left : left + width] += dot_nn(rounded_ref[e * blk_dev // edges], part[e])
        left += width
    own_ref[:, :, at:] = acc_ref[:blk_dev, :, at:]
    send_ref[:, :, at:] = acc_ref[blk_dev:, :, at:].astype(jnp.bfloat16)


def turned_terms(target, rounded, parts, early=()):
    blk_dev, vecs, _ = rounded.shape
    shape = (blk_dev, vecs, sum(part.shape[2] for part in [*early[:1], *parts]))
    return pl.pallas_call(
        functools.partial(turned_kernel, len(parts)),
        out_shape=(jax.ShapeDtypeStruct(shape, jnp.float32), jax.ShapeDtypeStruct(shape, jnp.bfloat16)),
        in_specs=[VMEM_WHOLE] + [VMEM_WHOLE] * (1 + len(parts) + len(early)),
        out_specs=(VMEM_WHOLE, VMEM_WHOLE),
        scratch_shapes=[pltpu.VMEM((2 * blk_dev, *shape[1:]), jnp.float32)],
        compiler_params=pltpu.CompilerParams(vmem_limit_bytes=16 * MIB),
        cost_estimate=product_cost(parts, vecs),
        name="turned",
    )(target, rounded, *parts, *early)


def direct_kernel(target_ref, rounded_ref, following_ref, own_ref, *refs):
    mirrors, (out_ref, picked_ref) = refs[:-2], refs[-2:]
    targets = [target_ref[...][e, 0] for e in range(mirrors[0].shape[0])]
    blk_dev = rounded_ref.shape[0]
    edges = mirrors[0].shape[0]
    slots = edges // blk_dev
    picked_ref[:blk_dev] = rounded_ref[...]
    picked_ref[blk_dev:] = following_ref[...]
    for b in range(blk_dev):
        total = own_ref[b]
        for e in range(b * slots, (b + 1) * slots):
            left = 0
            for mirror in mirrors:
                width = mirror.shape[1]
                total += dot_nn(picked_ref[targets[e], :, left : left + width], mirror[e])
                left += width
        out_ref[b] = total


def direct_terms(target, rounded, following, own, mirrors):
    blk_dev, vecs, orbs = rounded.shape
    return pl.pallas_call(
        direct_kernel,
        out_shape=jax.ShapeDtypeStruct(rounded.shape, jnp.float32),
        in_specs=[VMEM_WHOLE] + [VMEM_WHOLE] * (3 + len(mirrors)),
        out_specs=VMEM_WHOLE,
        scratch_shapes=[pltpu.VMEM((2 * blk_dev, vecs, orbs), jnp.bfloat16)],
        compiler_params=pltpu.CompilerParams(vmem_limit_bytes=16 * MIB),
        cost_estimate=product_cost(mirrors, vecs),
        name="direct",
    )(target, rounded, following, own, *mirrors)


def mirror_kernel(tiles_ref, after_ref, out_ref):
    for e in range(tiles_ref.shape[0]):
        out_ref[e] = tiles_ref[e].T


def mirrored(tiles, after):
    edges, rows, width = tiles.shape
    return pl.pallas_call(
        mirror_kernel,
        out_shape=jax.ShapeDtypeStruct((edges, width, rows), tiles.dtype),
        in_specs=[VMEM_WHOLE, pl.BlockSpec(memory_space=pl.ANY)],
        out_specs=VMEM_WHOLE,
        compiler_params=pltpu.CompilerParams(vmem_limit_bytes=16 * MIB),
        cost_estimate=pl.CostEstimate(flops=tiles.size * 400, bytes_accessed=4 * tiles.size, transcendentals=0),
        name="mirror",
    )(tiles, after)


def rounded_kernel(direct_ref, arrive_ref, previous_ref, rounded_ref):
    panel = 2.0 * (direct_ref[...] + arrive_ref[...].astype(jnp.float32)) - previous_ref[...]
    rounded_ref[...] = panel.astype(jnp.bfloat16)


def rounded_update(direct, arrive, previous):
    return pl.pallas_call(
        rounded_kernel,
        out_shape=jax.ShapeDtypeStruct(direct.shape, jnp.bfloat16),
        in_specs=[VMEM_WHOLE] * 3,
        out_specs=VMEM_WHOLE,
        compiler_params=pltpu.CompilerParams(vmem_limit_bytes=16 * MIB),
        name="rounded",
    )(direct, arrive, previous)


def exchanged(tiles):
    return lax.all_to_all(tiles, "gx", split_axis=0, concat_axis=0, tiled=True)


def per_device(edge_tiles, trial_panel, col_blocks):
    blk_dev, _, orbs = trial_panel.shape
    tiles, rows, _ = edge_tiles.shape
    group = lax.axis_size("gx")
    block_total = blk_dev * group
    domain = lax.axis_index("gx")
    own_cols = lax.dynamic_slice_in_dim(col_blocks, domain * blk_dev, blk_dev, 0).reshape(-1)
    target = jnp.mod(own_cols - domain * blk_dev, block_total)
    padded = jnp.pad(target, (0, -target.size % SUBLANES))
    target = jnp.broadcast_to(padded[:, None], (padded.size, LANES))
    rounded = trial_panel.astype(jnp.bfloat16)
    fits = tiles // group == QUAD and rows % QUAD == 0
    if fits and orbs % LANES == LANES // 2 and orbs % (4 * QUAD * QUAD) == 0:
        cuts = [(0, orbs)]
        parts = [unpack(exchanged(pack(edge_tiles, *cut)), rows, orbs, cut[1]) for cut in cuts]
    else:
        parts = [lax.all_to_all(edge_tiles, "gx", split_axis=0, concat_axis=1, tiled=True)]
    early = turned_terms(target, rounded, parts[:1]) if len(parts) > 1 else ()
    mirrors = [mirrored(part, early[1]) for part in parts[:-1]]

    previous, current = None, trial_panel
    for k in range(DEGREE):
        following = passed_along(rounded, "gx", -1)
        if k == 0:
            own, send = turned_terms(target, rounded, parts[len(parts) - 1 :], early)
            mirrors.append(mirrored(parts[-1], send))
        else:
            own, send = turned_terms(target, rounded, parts)
        arrive = passed_along(send, "gx", 1)
        direct = direct_terms(target, rounded, following, own, mirrors)
        if k == 0:
            total = direct + arrive.astype(jnp.float32)
            rounded = total.astype(jnp.bfloat16)
        else:
            if k == DEGREE - 2:
                rounded = rounded_update(direct, arrive, previous)
                direct, arrive, previous, rounded = lax.optimization_barrier((direct, arrive, previous, rounded))
            total = 2.0 * (direct + arrive.astype(jnp.float32)) - previous
            if k < DEGREE - 2:
                rounded = total.astype(jnp.bfloat16)
        previous, current = current, total
    return previous, current


def solution(mesh):
    return jax.shard_map(
        per_device,
        mesh=mesh,
        in_specs=(P("member", "gx", None), P(("member", "gx"), None, None), P()),
        out_specs=(P(("member", "gx"), None, None), P(("member", "gx"), None, None)),
        check_vma=False,
    )
```

```python
import functools

import jax
import jax.numpy as jnp
from jax import lax
from jax.experimental import pallas as pl
from jax.experimental.pallas import tpu as pltpu
from jax.sharding import PartitionSpec as P

DEGREE = 4
LANES = 128
QUAD = 4
MIB = 2**20
VMEM_WHOLE = pl.BlockSpec(memory_space=pltpu.VMEM)
HBM_WHOLE = pl.BlockSpec(memory_space=pltpu.HBM)
SUBLANES = 8


def passed_along(value, axis, steps):
    count = lax.axis_size(axis)
    pairs = [(source, (source + steps) % count) for source in range(count)]
    return lax.ppermute(value, axis, pairs)


def dot_nn(a, b):
    return lax.dot_general(a, b, (((1,), (0,)), ((), ())), preferred_element_type=jnp.float32)


def dot_nt(a, b):
    return lax.dot_general(a, b, (((1,), (1,)), ((), ())), preferred_element_type=jnp.float32)


def selector(rows, columns, source_of_row):
    row = lax.broadcasted_iota(jnp.int32, (rows, columns), 0)
    column = lax.broadcasted_iota(jnp.int32, (rows, columns), 1)
    return (column == source_of_row(row)).astype(jnp.bfloat16)


def pack_kernel(left, bounds, x_ref, out_ref, x_buf, out_buf, tail_buf, in_sems, out_sems):
    rows, tiles, width = x_buf.shape
    group = tiles // QUAD
    unit = QUAD * QUAD
    steps = rows // QUAD
    full = width // LANES
    half = LANES // 2
    has_tail = width % LANES > 0
    length = steps * unit
    arrivals = []
    for stage, (start, stop) in enumerate(zip(bounds[:-1], bounds[1:])):
        part = pl.ds(start * QUAD, (stop - start) * QUAD)
        arrivals.append(
            pltpu.make_async_copy(x_ref.at[part, :, pl.ds(left, width)], x_buf.at[part], in_sems.at[stage])
        )
        arrivals[-1].start()
    order = selector(QUAD * tiles, QUAD * tiles, lambda o: ((o % unit) // QUAD) * tiles + (o // unit) * QUAD + o % QUAD)
    leaving = []

    def leave(first, count):
        part = pl.ds(first, count)
        copy = pltpu.make_async_copy(out_buf.at[:, part, :], out_ref.at[:, part, :], out_sems.at[len(leaving)])
        copy.start()
        leaving.append(copy)

    begun = 0
    for j in range(steps):
        if j in bounds:
            arrivals[bounds.index(j)].wait()
        data = x_buf[j * QUAD : (j + 1) * QUAD].reshape(QUAD * tiles, width)
        for at in range(0, full * LANES, 2 * LANES):
            wide = min(2 * LANES, full * LANES - at)
            part = dot_nn(order, data[:, at : at + wide]).astype(jnp.bfloat16)
            for k in range(0, wide, LANES):
                first = (at + k) // LANES * length + j * unit
                out_buf[:, first : first + unit, :] = part[:, k : k + LANES].reshape(group, unit, LANES)
        if has_tail:
            last = dot_nn(order, data[:, full * LANES :]).reshape(group, unit, half)
            both = jnp.concatenate([last[:, : unit // 2], last[:, unit // 2 :]], axis=2)
            tail_buf[:, j * unit // 2 : (j + 1) * unit // 2, :] = both
        if j + 1 in bounds:
            for k in range(full):
                leave(k * length + begun * unit, (j + 1 - begun) * unit)
            begun = j + 1
    if has_tail:
        out_buf[:, full * length :, :] = tail_buf[...].astype(jnp.bfloat16)
        leave(full * length, length // 2)
    for copy in leaving:
        copy.wait()


def pack(edge_tiles, left, width):
    tiles, rows, _ = edge_tiles.shape
    group = tiles // QUAD
    turned = jnp.transpose(edge_tiles, (1, 0, 2))
    flat = rows * QUAD * width // LANES
    steps = rows // QUAD
    bounds = tuple(sorted({0, -(-3 * steps // 8), -(-6 * steps // 8), steps}))
    stages = len(bounds) - 1
    return pl.pallas_call(
        functools.partial(pack_kernel, left, bounds),
        out_shape=jax.ShapeDtypeStruct((group, flat, LANES), jnp.bfloat16),
        in_specs=[HBM_WHOLE],
        out_specs=HBM_WHOLE,
        scratch_shapes=[
            pltpu.VMEM((rows, tiles, width), jnp.bfloat16),
            pltpu.VMEM((group, flat, LANES), jnp.bfloat16),
            pltpu.VMEM((group, rows * QUAD // 2, LANES), jnp.float32),
            pltpu.SemaphoreType.DMA((stages,)),
            pltpu.SemaphoreType.DMA((stages * (width // LANES) + 1,)),
        ],
        compiler_params=pltpu.CompilerParams(vmem_limit_bytes=58 * MIB),
        cost_estimate=pl.CostEstimate(
            flops=2 * rows * tiles * width * 4 * tiles, bytes_accessed=4 * rows * tiles * width, transcendentals=0
        ),
        name="pack",
    )(turned)


def unpack_kernel(rows, in_ref, out_ref):
    _, orbs, width = out_ref.shape
    full = width // LANES
    half = LANES // 2
    unit = QUAD * QUAD
    block = 4 * QUAD
    size = block * unit
    span = block * QUAD
    order = selector(size, size, lambda o: (o % span) // QUAD * unit + (o % QUAD) * QUAD + o // span)
    order_tail = selector(
        size, size // 2, lambda o: (o % span) // QUAD * (unit // 2) + (o % QUAD) % 2 * QUAD + o // span
    )
    early = lax.broadcasted_iota(jnp.int32, (size, half), 0) % QUAD < 2

    def lane_block(j, start, stop, scale):
        held = rows // scale
        pieces = []
        while start < stop:
            g, at = divmod(start, held)
            count = min(stop - start, held - at)
            pieces.append(in_ref[g, j * rows + at : j * rows + at + count, :])
            start += count
        return pieces[0] if len(pieces) == 1 else jnp.concatenate(pieces, axis=0)

    for i in range(orbs // span):
        for at in range(0, full, 2):
            wide = range(at, min(at + 2, full))
            data = jnp.concatenate([lane_block(j, i * size, (i + 1) * size, 1) for j in wide], axis=1)
            clean = dot_nn(order, data).astype(jnp.bfloat16)
            for e in range(QUAD):
                place = slice(at * LANES, (at + len(wide)) * LANES)
                out_ref[e, pl.ds(i * span, span), place] = clean[e * span : (e + 1) * span]
        if width % LANES:
            both = dot_nn(order_tail, lane_block(full, i * size // 2, (i + 1) * size // 2, 2))
            last = jnp.where(early, both[:, :half], both[:, half:]).astype(jnp.bfloat16)
            for e in range(QUAD):
                out_ref[e, pl.ds(i * span, span), full * LANES :] = last[e * span : (e + 1) * span]


def unpack(arrived, rows, orbs, width):
    return pl.pallas_call(
        functools.partial(unpack_kernel, rows * QUAD),
        out_shape=jax.ShapeDtypeStruct((QUAD, orbs, width), jnp.bfloat16),
        in_specs=[VMEM_WHOLE],
        out_specs=VMEM_WHOLE,
        compiler_params=pltpu.CompilerParams(vmem_limit_bytes=16 * MIB),
        cost_estimate=pl.CostEstimate(
            flops=2 * QUAD * orbs * width * 256, bytes_accessed=4 * QUAD * orbs * width, transcendentals=0
        ),
        name="unpack",
    )(arrived)


def product_cost(tiles, vecs):
    return pl.CostEstimate(flops=8 * tiles.size * vecs, bytes_accessed=2 * tiles.size, transcendentals=0)


def spread_panels(rounded, rows, bounds):
    blk_dev, vecs, orbs = rounded.shape
    repeated = jnp.repeat(rounded, QUAD // blk_dev, axis=0).reshape(QUAD * vecs, orbs)

    def spread(first, count, unit, offset):
        row = jnp.arange(count)[None, :]
        source = first + row // unit * QUAD + offset + row % unit // QUAD
        place = (jnp.arange(orbs)[:, None] == source).astype(jnp.bfloat16)
        mine = jnp.arange(QUAD * vecs)[:, None] // vecs == row % QUAD
        wide = jnp.dot(repeated, place, preferred_element_type=jnp.float32)
        return jnp.where(mine, wide, 0.0).astype(jnp.bfloat16)

    panels = []
    for start, stop in zip(bounds[:-1], bounds[1:]):
        first, count = start * rows, (stop - start) * rows * QUAD
        panels.append(spread(first, count, QUAD * QUAD, 0))
        panels.append(spread(first, count // 2, QUAD * QUAD // 2, 0))
        panels.append(spread(first, count // 2, QUAD * QUAD // 2, QUAD // 2))
    return panels


def first_turned_kernel(rows, bounds, target_ref, from_ref, *refs):
    panels, (own_ref, send_ref, packed_ref, acc_ref, spread_ref, sems) = refs[:-6], refs[-6:]
    targets = [target_ref[...][e, 0] for e in range(QUAD)]
    blk_dev, vecs, orbs = own_ref.shape
    full = orbs // LANES
    half = LANES // 2
    arrivals = []
    for stage, (start, stop) in enumerate(zip(bounds[:-1], bounds[1:])):
        part = pl.ds(start, stop - start)
        arrivals.append(pltpu.make_async_copy(from_ref.at[part], packed_ref.at[part], sems.at[stage]))
        arrivals[-1].start()
    for stage, (start, stop) in enumerate(zip(bounds[:-1], bounds[1:])):
        arrivals[stage].wait()
        whole, early, late = (panel[...] for panel in panels[3 * stage : 3 * stage + 3])

        def add(place, part, stage=stage):
            if stage == 0:
                acc_ref[:, place] = part
            else:
                acc_ref[:, place] += part

        for at in range(0, full, 2):
            wide = range(at, min(at + 2, full))
            data = [packed_ref[start:stop, j * rows : (j + 1) * rows, :].reshape(-1, LANES) for j in wide]
            add(slice(at * LANES, (at + len(wide)) * LANES), dot_nn(whole, jnp.concatenate(data, axis=1)))
        tail = jnp.concatenate([packed_ref[g, full * rows :, :] for g in range(start, stop)], axis=0)
        add(slice(full * LANES, orbs), dot_nn(early, tail)[:, :half] + dot_nn(late, tail)[:, half:])
    spread_ref[...] = jnp.zeros_like(spread_ref)
    for e in range(QUAD):
        spread_ref[targets[e]] += acc_ref[e * vecs : (e + 1) * vecs]
    own_ref[...] = spread_ref[:blk_dev]
    send_ref[...] = spread_ref[blk_dev:].astype(jnp.bfloat16)


def first_turned(target, rounded, arrived, rows):
    blk_dev, vecs, orbs = rounded.shape
    group = arrived.shape[0]
    bounds = (0, group // 2, group)
    panels = spread_panels(rounded, rows, bounds)
    return pl.pallas_call(
        functools.partial(first_turned_kernel, rows * QUAD, bounds),
        out_shape=(
            jax.ShapeDtypeStruct(rounded.shape, jnp.float32),
            jax.ShapeDtypeStruct(rounded.shape, jnp.bfloat16),
            jax.ShapeDtypeStruct(arrived.shape, arrived.dtype),
        ),
        in_specs=[VMEM_WHOLE, HBM_WHOLE] + [VMEM_WHOLE] * len(panels),
        out_specs=(VMEM_WHOLE,) * 3,
        scratch_shapes=[
            pltpu.VMEM((QUAD * vecs, orbs), jnp.float32),
            pltpu.VMEM((2 * blk_dev, vecs, orbs), jnp.float32),
            pltpu.SemaphoreType.DMA((len(bounds) - 1,)),
        ],
        compiler_params=pltpu.CompilerParams(vmem_limit_bytes=20 * MIB),
        cost_estimate=pl.CostEstimate(
            flops=8 * arrived.size * vecs, bytes_accessed=2 * arrived.size, transcendentals=0
        ),
        name="first_turned",
    )(target, arrived, *panels)


def turned_kernel(target_ref, rounded_ref, tiles_ref, own_ref, send_ref, acc_ref):
    targets = [target_ref[...][e, 0] for e in range(tiles_ref.shape[0])]
    blk_dev = rounded_ref.shape[0]
    edges = tiles_ref.shape[0]
    acc_ref[...] = jnp.zeros_like(acc_ref)
    for e in range(edges):
        acc_ref[targets[e]] += dot_nn(rounded_ref[e * blk_dev // edges], tiles_ref[e])
    own_ref[...] = acc_ref[:blk_dev]
    send_ref[...] = acc_ref[blk_dev:].astype(jnp.bfloat16)


def turned_terms(target, rounded, tiles):
    blk_dev, vecs, orbs = rounded.shape
    return pl.pallas_call(
        turned_kernel,
        out_shape=(
            jax.ShapeDtypeStruct(rounded.shape, jnp.float32),
            jax.ShapeDtypeStruct(rounded.shape, jnp.bfloat16),
        ),
        in_specs=[VMEM_WHOLE] * 3,
        out_specs=(VMEM_WHOLE, VMEM_WHOLE),
        scratch_shapes=[pltpu.VMEM((2 * blk_dev, vecs, orbs), jnp.float32)],
        compiler_params=pltpu.CompilerParams(vmem_limit_bytes=16 * MIB),
        cost_estimate=product_cost(tiles, vecs),
        name="turned",
    )(target, rounded, tiles)


def direct_kernel(product, target_ref, rounded_ref, following_ref, own_ref, tiles_ref, out_ref, picked_ref):
    targets = [target_ref[...][e, 0] for e in range(tiles_ref.shape[0])]
    blk_dev = rounded_ref.shape[0]
    edges = tiles_ref.shape[0]
    slots = edges // blk_dev
    picked_ref[:blk_dev] = rounded_ref[...]
    picked_ref[blk_dev:] = following_ref[...]
    for b in range(blk_dev):
        total = own_ref[b]
        for e in range(b * slots, (b + 1) * slots):
            total += product(picked_ref[targets[e]], tiles_ref[e])
        out_ref[b] = total


def direct_terms(target, rounded, following, own, tiles, product):
    blk_dev, vecs, orbs = rounded.shape
    return pl.pallas_call(
        functools.partial(direct_kernel, product),
        out_shape=jax.ShapeDtypeStruct(rounded.shape, jnp.float32),
        in_specs=[VMEM_WHOLE] + [VMEM_WHOLE] * 4,
        out_specs=VMEM_WHOLE,
        scratch_shapes=[pltpu.VMEM((2 * blk_dev, vecs, orbs), jnp.bfloat16)],
        compiler_params=pltpu.CompilerParams(vmem_limit_bytes=16 * MIB),
        cost_estimate=product_cost(tiles, vecs),
        name="direct",
    )(target, rounded, following, own, tiles)


def mirror_kernel(tiles_ref, after_ref, out_ref):
    for e in range(tiles_ref.shape[0]):
        out_ref[e] = tiles_ref[e].T


def mirrored(tiles, after):
    edges, rows, width = tiles.shape
    return pl.pallas_call(
        mirror_kernel,
        out_shape=jax.ShapeDtypeStruct((edges, width, rows), tiles.dtype),
        in_specs=[VMEM_WHOLE, pl.BlockSpec(memory_space=pl.ANY)],
        out_specs=VMEM_WHOLE,
        compiler_params=pltpu.CompilerParams(vmem_limit_bytes=16 * MIB),
        cost_estimate=pl.CostEstimate(flops=tiles.size * 400, bytes_accessed=4 * tiles.size, transcendentals=0),
        name="mirror",
    )(tiles, after)


def rounded_kernel(direct_ref, arrive_ref, previous_ref, rounded_ref):
    panel = 2.0 * (direct_ref[...] + arrive_ref[...].astype(jnp.float32)) - previous_ref[...]
    rounded_ref[...] = panel.astype(jnp.bfloat16)


def rounded_update(direct, arrive, previous):
    return pl.pallas_call(
        rounded_kernel,
        out_shape=jax.ShapeDtypeStruct(direct.shape, jnp.bfloat16),
        in_specs=[VMEM_WHOLE] * 3,
        out_specs=VMEM_WHOLE,
        compiler_params=pltpu.CompilerParams(vmem_limit_bytes=16 * MIB),
        name="rounded",
    )(direct, arrive, previous)


def final_kernel(direct_ref, arrive_ref, previous_ref, out_ref, panel_ref, sems):
    copies = []
    for b in range(panel_ref.shape[0]):
        panel_ref[b] = 2.0 * (direct_ref[b] + arrive_ref[b].astype(jnp.float32)) - previous_ref[b]
        copies.append(pltpu.make_async_copy(panel_ref.at[b], out_ref.at[b], sems.at[b]))
        copies[-1].start()
    for copy in copies:
        copy.wait()


def final_update(direct, arrive, previous):
    return pl.pallas_call(
        final_kernel,
        out_shape=jax.ShapeDtypeStruct(direct.shape, jnp.float32),
        in_specs=[VMEM_WHOLE] * 3,
        out_specs=HBM_WHOLE,
        scratch_shapes=[pltpu.VMEM(direct.shape, jnp.float32), pltpu.SemaphoreType.DMA(direct.shape[:1])],
        compiler_params=pltpu.CompilerParams(vmem_limit_bytes=16 * MIB),
        name="final",
    )(direct, arrive, previous)


def exchanged(tiles):
    return lax.all_to_all(tiles, "gx", split_axis=0, concat_axis=0, tiled=True)


def per_device(edge_tiles, trial_panel, col_blocks):
    blk_dev, _, orbs = trial_panel.shape
    tiles, rows, _ = edge_tiles.shape
    group = lax.axis_size("gx")
    block_total = blk_dev * group
    domain = lax.axis_index("gx")
    own_cols = lax.dynamic_slice_in_dim(col_blocks, domain * blk_dev, blk_dev, 0).reshape(-1)
    target = jnp.mod(own_cols - domain * blk_dev, block_total)
    padded = jnp.pad(target, (0, -target.size % SUBLANES))
    target = jnp.broadcast_to(padded[:, None], (padded.size, LANES))
    rounded = trial_panel.astype(jnp.bfloat16)
    fits = tiles // group == QUAD and QUAD % blk_dev == 0 and rows % QUAD == 0 and group % 8 == 0
    following = passed_along(rounded, "gx", -1)
    if fits and orbs % LANES == LANES // 2 and orbs % (4 * QUAD * QUAD) == 0:
        own, send, packed = first_turned(target, rounded, exchanged(pack(edge_tiles, 0, orbs)), rows)
        arrive = passed_along(send, "gx", 1)
        owned = unpack(packed, rows, orbs, orbs)
    else:
        owned = lax.all_to_all(edge_tiles, "gx", split_axis=0, concat_axis=1, tiled=True)
        own, send = turned_terms(target, rounded, owned)
        arrive = passed_along(send, "gx", 1)
    direct = direct_terms(target, rounded, following, own, owned, dot_nt)
    mirror = mirrored(owned, direct)
    previous, current = trial_panel, direct + arrive.astype(jnp.float32)
    rounded = current.astype(jnp.bfloat16)
    for k in range(1, DEGREE):
        following = passed_along(rounded, "gx", -1)
        own, send = turned_terms(target, rounded, owned)
        arrive = passed_along(send, "gx", 1)
        direct = direct_terms(target, rounded, following, own, mirror, dot_nn)
        if k == DEGREE - 2:
            rounded = rounded_update(direct, arrive, previous)
            direct, arrive, previous, rounded = lax.optimization_barrier((direct, arrive, previous, rounded))
        if k < DEGREE - 1:
            total = 2.0 * (direct + arrive.astype(jnp.float32)) - previous
        else:
            total = final_update(direct, arrive, previous)
        if k < DEGREE - 2:
            rounded = total.astype(jnp.bfloat16)
        previous, current = current, total
    return previous, current


def solution(mesh):
    return jax.shard_map(
        per_device,
        mesh=mesh,
        in_specs=(P("member", "gx", None), P(("member", "gx"), None, None), P()),
        out_specs=(P(("member", "gx"), None, None), P(("member", "gx"), None, None)),
        check_vma=False,
    )
```

```python
import functools

import jax
import jax.numpy as jnp
from jax import lax
from jax.experimental import pallas as pl
from jax.experimental.pallas import tpu as pltpu
from jax.sharding import PartitionSpec as P

DEGREE = 4
LANES = 128
QUAD = 4
MIB = 2**20
VMEM_WHOLE = pl.BlockSpec(memory_space=pltpu.VMEM)
HBM_WHOLE = pl.BlockSpec(memory_space=pltpu.HBM)
SUBLANES = 8


def passed_along(value, axis, steps):
    count = lax.axis_size(axis)
    pairs = [(source, (source + steps) % count) for source in range(count)]
    return lax.ppermute(value, axis, pairs)


def dot_nn(a, b):
    return lax.dot_general(a, b, (((1,), (0,)), ((), ())), preferred_element_type=jnp.float32)


def dot_nt(a, b):
    return lax.dot_general(a, b, (((1,), (1,)), ((), ())), preferred_element_type=jnp.float32)


def selector(rows, columns, source_of_row):
    row = lax.broadcasted_iota(jnp.int32, (rows, columns), 0)
    column = lax.broadcasted_iota(jnp.int32, (rows, columns), 1)
    return (column == source_of_row(row)).astype(jnp.bfloat16)


def dense_rows(blk_dev, vecs, orbs):
    return blk_dev * vecs * orbs // LANES


def store_dense(ref, panels):
    vecs, orbs = panels[0].shape
    full = orbs // LANES
    for c, panel in enumerate(panels):
        for j in range(full):
            first = (j * len(panels) + c) * vecs
            ref[first : first + vecs, :] = panel[:, j * LANES : (j + 1) * LANES].astype(ref.dtype)
    ends = jnp.concatenate([panel[:, full * LANES :] for panel in panels], axis=1)
    ref[full * len(panels) * vecs :, :] = ends.astype(ref.dtype)


def load_dense(ref, c, shape):
    blk_dev, vecs, orbs = shape
    full = orbs // LANES
    blocks = [ref[(j * blk_dev + c) * vecs : (j * blk_dev + c + 1) * vecs, :].astype(jnp.float32) for j in range(full)]
    width = orbs % LANES
    ends = ref[full * blk_dev * vecs :, :].astype(jnp.float32)
    return jnp.concatenate([*blocks, ends[:, c * width : (c + 1) * width]], axis=1)


def pack_kernel(left, bounds, x_ref, out_ref, x_buf, out_buf, tail_buf, in_sems, out_sems):
    rows, tiles, width = x_buf.shape
    group = tiles // QUAD
    unit = QUAD * QUAD
    steps = rows // QUAD
    full = width // LANES
    half = LANES // 2
    has_tail = width % LANES > 0
    length = steps * unit
    arrivals = []
    for stage, (start, stop) in enumerate(zip(bounds[:-1], bounds[1:])):
        part = pl.ds(start * QUAD, (stop - start) * QUAD)
        arrivals.append(
            pltpu.make_async_copy(x_ref.at[part, :, pl.ds(left, width)], x_buf.at[part], in_sems.at[stage])
        )
        arrivals[-1].start()
    order = selector(QUAD * tiles, QUAD * tiles, lambda o: ((o % unit) // QUAD) * tiles + (o // unit) * QUAD + o % QUAD)
    leaving = []

    def leave(first, count):
        part = pl.ds(first, count)
        copy = pltpu.make_async_copy(out_buf.at[:, part, :], out_ref.at[:, part, :], out_sems.at[len(leaving)])
        copy.start()
        leaving.append(copy)

    begun = 0
    for j in range(steps):
        if j in bounds:
            arrivals[bounds.index(j)].wait()
        data = x_buf[j * QUAD : (j + 1) * QUAD].reshape(QUAD * tiles, width)
        for at in range(0, full * LANES, 2 * LANES):
            wide = min(2 * LANES, full * LANES - at)
            part = dot_nn(order, data[:, at : at + wide]).astype(jnp.bfloat16)
            for k in range(0, wide, LANES):
                first = (at + k) // LANES * length + j * unit
                out_buf[:, first : first + unit, :] = part[:, k : k + LANES].reshape(group, unit, LANES)
        if has_tail:
            last = dot_nn(order, data[:, full * LANES :]).reshape(group, unit, half)
            both = jnp.concatenate([last[:, : unit // 2], last[:, unit // 2 :]], axis=2)
            tail_buf[:, j * unit // 2 : (j + 1) * unit // 2, :] = both
        if j + 1 in bounds:
            for k in range(full):
                leave(k * length + begun * unit, (j + 1 - begun) * unit)
            begun = j + 1
    if has_tail:
        out_buf[:, full * length :, :] = tail_buf[...].astype(jnp.bfloat16)
        leave(full * length, length // 2)
    for copy in leaving:
        copy.wait()


def pack(edge_tiles, left, width):
    tiles, rows, _ = edge_tiles.shape
    group = tiles // QUAD
    turned = jnp.transpose(edge_tiles, (1, 0, 2))
    flat = rows * QUAD * width // LANES
    steps = rows // QUAD
    bounds = tuple(sorted({0, -(-3 * steps // 8), -(-6 * steps // 8), steps}))
    stages = len(bounds) - 1
    return pl.pallas_call(
        functools.partial(pack_kernel, left, bounds),
        out_shape=jax.ShapeDtypeStruct((group, flat, LANES), jnp.bfloat16),
        in_specs=[HBM_WHOLE],
        out_specs=HBM_WHOLE,
        scratch_shapes=[
            pltpu.VMEM((rows, tiles, width), jnp.bfloat16),
            pltpu.VMEM((group, flat, LANES), jnp.bfloat16),
            pltpu.VMEM((group, rows * QUAD // 2, LANES), jnp.float32),
            pltpu.SemaphoreType.DMA((stages,)),
            pltpu.SemaphoreType.DMA((stages * (width // LANES) + 1,)),
        ],
        compiler_params=pltpu.CompilerParams(vmem_limit_bytes=58 * MIB),
        cost_estimate=pl.CostEstimate(
            flops=2 * rows * tiles * width * 4 * tiles, bytes_accessed=4 * rows * tiles * width, transcendentals=0
        ),
        name="pack",
    )(turned)


def unpack_kernel(rows, in_ref, out_ref):
    _, orbs, width = out_ref.shape
    full = width // LANES
    half = LANES // 2
    unit = QUAD * QUAD
    block = 4 * QUAD
    size = block * unit
    span = block * QUAD
    order = selector(size, size, lambda o: (o % span) // QUAD * unit + (o % QUAD) * QUAD + o // span)
    order_tail = selector(
        size, size // 2, lambda o: (o % span) // QUAD * (unit // 2) + (o % QUAD) % 2 * QUAD + o // span
    )
    early = lax.broadcasted_iota(jnp.int32, (size, half), 0) % QUAD < 2

    def lane_block(j, start, stop, scale):
        held = rows // scale
        pieces = []
        while start < stop:
            g, at = divmod(start, held)
            count = min(stop - start, held - at)
            pieces.append(in_ref[g, j * rows + at : j * rows + at + count, :])
            start += count
        return pieces[0] if len(pieces) == 1 else jnp.concatenate(pieces, axis=0)

    for i in range(orbs // span):
        for at in range(0, full, 2):
            wide = range(at, min(at + 2, full))
            data = jnp.concatenate([lane_block(j, i * size, (i + 1) * size, 1) for j in wide], axis=1)
            clean = dot_nn(order, data).astype(jnp.bfloat16)
            for e in range(QUAD):
                place = slice(at * LANES, (at + len(wide)) * LANES)
                out_ref[e, pl.ds(i * span, span), place] = clean[e * span : (e + 1) * span]
        if width % LANES:
            both = dot_nn(order_tail, lane_block(full, i * size // 2, (i + 1) * size // 2, 2))
            last = jnp.where(early, both[:, :half], both[:, half:]).astype(jnp.bfloat16)
            for e in range(QUAD):
                out_ref[e, pl.ds(i * span, span), full * LANES :] = last[e * span : (e + 1) * span]


def unpack(arrived, rows, orbs, width):
    return pl.pallas_call(
        functools.partial(unpack_kernel, rows * QUAD),
        out_shape=jax.ShapeDtypeStruct((QUAD, orbs, width), jnp.bfloat16),
        in_specs=[VMEM_WHOLE],
        out_specs=VMEM_WHOLE,
        compiler_params=pltpu.CompilerParams(vmem_limit_bytes=16 * MIB),
        cost_estimate=pl.CostEstimate(
            flops=2 * QUAD * orbs * width * 256, bytes_accessed=4 * QUAD * orbs * width, transcendentals=0
        ),
        name="unpack",
    )(arrived)


def product_cost(tiles, vecs):
    return pl.CostEstimate(flops=8 * tiles.size * vecs, bytes_accessed=2 * tiles.size, transcendentals=0)


def spread_panels(rounded, rows, bounds):
    blk_dev, vecs, orbs = rounded.shape
    repeated = jnp.repeat(rounded, QUAD // blk_dev, axis=0).reshape(QUAD * vecs, orbs)

    def spread(first, count, unit, offset):
        row = jnp.arange(count)[None, :]
        source = first + row // unit * QUAD + offset + row % unit // QUAD
        place = (jnp.arange(orbs)[:, None] == source).astype(jnp.bfloat16)
        mine = jnp.arange(QUAD * vecs)[:, None] // vecs == row % QUAD
        wide = jnp.dot(repeated, place, preferred_element_type=jnp.float32)
        return jnp.where(mine, wide, 0.0).astype(jnp.bfloat16)

    panels = []
    for start, stop in zip(bounds[:-1], bounds[1:]):
        first, count = start * rows, (stop - start) * rows * QUAD
        panels.append(spread(first, count, QUAD * QUAD, 0))
        panels.append(spread(first, count // 2, QUAD * QUAD // 2, 0))
        panels.append(spread(first, count // 2, QUAD * QUAD // 2, QUAD // 2))
    return panels


def first_turned_kernel(rows, bounds, target_ref, from_ref, *refs):
    panels, (own_ref, send_ref, packed_ref, acc_ref, spread_ref, sems) = refs[:-6], refs[-6:]
    targets = [target_ref[...][e, 0] for e in range(QUAD)]
    blk_dev, vecs, orbs = own_ref.shape
    full = orbs // LANES
    half = LANES // 2
    arrivals = []
    for stage, (start, stop) in enumerate(zip(bounds[:-1], bounds[1:])):
        part = pl.ds(start, stop - start)
        arrivals.append(pltpu.make_async_copy(from_ref.at[part], packed_ref.at[part], sems.at[stage]))
        arrivals[-1].start()
    for stage, (start, stop) in enumerate(zip(bounds[:-1], bounds[1:])):
        arrivals[stage].wait()
        whole, early, late = (panel[...] for panel in panels[3 * stage : 3 * stage + 3])

        def add(place, part, stage=stage):
            if stage == 0:
                acc_ref[:, place] = part
            else:
                acc_ref[:, place] += part

        for at in range(0, full, 2):
            wide = range(at, min(at + 2, full))
            data = [packed_ref[start:stop, j * rows : (j + 1) * rows, :].reshape(-1, LANES) for j in wide]
            add(slice(at * LANES, (at + len(wide)) * LANES), dot_nn(whole, jnp.concatenate(data, axis=1)))
        tail = jnp.concatenate([packed_ref[g, full * rows :, :] for g in range(start, stop)], axis=0)
        add(slice(full * LANES, orbs), dot_nn(early, tail)[:, :half] + dot_nn(late, tail)[:, half:])
    spread_ref[...] = jnp.zeros_like(spread_ref)
    for e in range(QUAD):
        spread_ref[targets[e]] += acc_ref[e * vecs : (e + 1) * vecs]
    own_ref[...] = spread_ref[:blk_dev]
    store_dense(send_ref, [spread_ref[blk_dev + c] for c in range(blk_dev)])


def first_turned(target, rounded, arrived, rows):
    blk_dev, vecs, orbs = rounded.shape
    group = arrived.shape[0]
    bounds = (0, group // 2, group)
    panels = spread_panels(rounded, rows, bounds)
    return pl.pallas_call(
        functools.partial(first_turned_kernel, rows * QUAD, bounds),
        out_shape=(
            jax.ShapeDtypeStruct(rounded.shape, jnp.float32),
            jax.ShapeDtypeStruct((dense_rows(*rounded.shape), LANES), jnp.bfloat16),
            jax.ShapeDtypeStruct(arrived.shape, arrived.dtype),
        ),
        in_specs=[VMEM_WHOLE, HBM_WHOLE] + [VMEM_WHOLE] * len(panels),
        out_specs=(VMEM_WHOLE,) * 3,
        scratch_shapes=[
            pltpu.VMEM((QUAD * vecs, orbs), jnp.float32),
            pltpu.VMEM((2 * blk_dev, vecs, orbs), jnp.float32),
            pltpu.SemaphoreType.DMA((len(bounds) - 1,)),
        ],
        compiler_params=pltpu.CompilerParams(vmem_limit_bytes=20 * MIB),
        cost_estimate=pl.CostEstimate(
            flops=8 * arrived.size * vecs, bytes_accessed=2 * arrived.size, transcendentals=0
        ),
        name="first_turned",
    )(target, arrived, *panels)


def turned_kernel(target_ref, rounded_ref, tiles_ref, own_ref, send_ref, acc_ref):
    targets = [target_ref[...][e, 0] for e in range(tiles_ref.shape[0])]
    blk_dev = rounded_ref.shape[0]
    edges = tiles_ref.shape[0]
    acc_ref[...] = jnp.zeros_like(acc_ref)
    for e in range(edges):
        acc_ref[targets[e]] += dot_nn(rounded_ref[e * blk_dev // edges], tiles_ref[e])
    own_ref[...] = acc_ref[:blk_dev]
    store_dense(send_ref, [acc_ref[blk_dev + c] for c in range(blk_dev)])


def turned_terms(target, rounded, tiles):
    blk_dev, vecs, orbs = rounded.shape
    return pl.pallas_call(
        turned_kernel,
        out_shape=(
            jax.ShapeDtypeStruct(rounded.shape, jnp.float32),
            jax.ShapeDtypeStruct((dense_rows(*rounded.shape), LANES), jnp.bfloat16),
        ),
        in_specs=[VMEM_WHOLE] * 3,
        out_specs=(VMEM_WHOLE, VMEM_WHOLE),
        scratch_shapes=[pltpu.VMEM((2 * blk_dev, vecs, orbs), jnp.float32)],
        compiler_params=pltpu.CompilerParams(vmem_limit_bytes=16 * MIB),
        cost_estimate=product_cost(tiles, vecs),
        name="turned",
    )(target, rounded, tiles)


def direct_kernel(product, target_ref, rounded_ref, following_ref, own_ref, tiles_ref, out_ref, picked_ref):
    targets = [target_ref[...][e, 0] for e in range(tiles_ref.shape[0])]
    blk_dev = rounded_ref.shape[0]
    edges = tiles_ref.shape[0]
    slots = edges // blk_dev
    picked_ref[:blk_dev] = rounded_ref[...]
    for c in range(blk_dev):
        picked_ref[blk_dev + c] = load_dense(following_ref, c, rounded_ref.shape).astype(jnp.bfloat16)
    for b in range(blk_dev):
        total = own_ref[b]
        for e in range(b * slots, (b + 1) * slots):
            total += product(picked_ref[targets[e]], tiles_ref[e])
        out_ref[b] = total


def direct_terms(target, rounded, following, own, tiles, product):
    blk_dev, vecs, orbs = rounded.shape
    return pl.pallas_call(
        functools.partial(direct_kernel, product),
        out_shape=jax.ShapeDtypeStruct(rounded.shape, jnp.float32),
        in_specs=[VMEM_WHOLE] + [VMEM_WHOLE] * 4,
        out_specs=VMEM_WHOLE,
        scratch_shapes=[pltpu.VMEM((2 * blk_dev, vecs, orbs), jnp.bfloat16)],
        compiler_params=pltpu.CompilerParams(vmem_limit_bytes=16 * MIB),
        cost_estimate=product_cost(tiles, vecs),
        name="direct",
    )(target, rounded, following, own, tiles)


def mirror_kernel(tiles_ref, after_ref, out_ref):
    for e in range(tiles_ref.shape[0]):
        out_ref[e] = tiles_ref[e].T


def mirrored(tiles, after):
    edges, rows, width = tiles.shape
    return pl.pallas_call(
        mirror_kernel,
        out_shape=jax.ShapeDtypeStruct((edges, width, rows), tiles.dtype),
        in_specs=[VMEM_WHOLE, pl.BlockSpec(memory_space=pl.ANY)],
        out_specs=VMEM_WHOLE,
        compiler_params=pltpu.CompilerParams(vmem_limit_bytes=16 * MIB),
        cost_estimate=pl.CostEstimate(flops=tiles.size * 400, bytes_accessed=4 * tiles.size, transcendentals=0),
        name="mirror",
    )(tiles, after)


def update_kernel(extra, total_out, first_ref, *refs):
    arrive, previous, outs = refs[: min(extra, 1)], refs[min(extra, 1) : extra], refs[extra:]
    shape = first_ref.shape
    panels = []
    for c in range(shape[0]):
        panel = first_ref[c]
        if arrive:
            panel = panel + load_dense(arrive[0], c, shape)
        if previous:
            panel = 2.0 * panel - previous[0][c]
        panels.append(panel)
        if total_out:
            outs[0][c] = panel
        if outs[total_out:]:
            outs[total_out][c] = panel.astype(jnp.bfloat16)
    if outs[total_out:]:
        store_dense(outs[total_out + 1], panels)


def updated(first, *rest, total=True, rounded=True):
    shapes = [jax.ShapeDtypeStruct(first.shape, jnp.float32)] if total else []
    if rounded:
        shapes.append(jax.ShapeDtypeStruct(first.shape, jnp.bfloat16))
        shapes.append(jax.ShapeDtypeStruct((dense_rows(*first.shape), LANES), jnp.bfloat16))
    return pl.pallas_call(
        functools.partial(update_kernel, len(rest), int(total)),
        out_shape=shapes,
        in_specs=[VMEM_WHOLE] * (1 + len(rest)),
        out_specs=[VMEM_WHOLE] * len(shapes),
        compiler_params=pltpu.CompilerParams(vmem_limit_bytes=16 * MIB),
        name="update",
    )(first, *rest)


def final_kernel(direct_ref, arrive_ref, previous_ref, out_ref, panel_ref, sems):
    copies = []
    for b in range(panel_ref.shape[0]):
        arrived = load_dense(arrive_ref, b, direct_ref.shape)
        panel_ref[b] = 2.0 * (direct_ref[b] + arrived) - previous_ref[b]
        copies.append(pltpu.make_async_copy(panel_ref.at[b], out_ref.at[b], sems.at[b]))
        copies[-1].start()
    for copy in copies:
        copy.wait()


def final_update(direct, arrive, previous):
    return pl.pallas_call(
        final_kernel,
        out_shape=jax.ShapeDtypeStruct(direct.shape, jnp.float32),
        in_specs=[VMEM_WHOLE] * 3,
        out_specs=HBM_WHOLE,
        scratch_shapes=[pltpu.VMEM(direct.shape, jnp.float32), pltpu.SemaphoreType.DMA(direct.shape[:1])],
        compiler_params=pltpu.CompilerParams(vmem_limit_bytes=16 * MIB),
        name="final",
    )(direct, arrive, previous)


def exchanged(tiles):
    return lax.all_to_all(tiles, "gx", split_axis=0, concat_axis=0, tiled=True)


def per_device(edge_tiles, trial_panel, col_blocks):
    blk_dev, _, orbs = trial_panel.shape
    tiles, rows, _ = edge_tiles.shape
    group = lax.axis_size("gx")
    block_total = blk_dev * group
    domain = lax.axis_index("gx")
    own_cols = lax.dynamic_slice_in_dim(col_blocks, domain * blk_dev, blk_dev, 0).reshape(-1)
    target = jnp.mod(own_cols - domain * blk_dev, block_total)
    padded = jnp.pad(target, (0, -target.size % SUBLANES))
    target = jnp.broadcast_to(padded[:, None], (padded.size, LANES))
    rounded, dense = updated(trial_panel, total=False)
    fits = tiles // group == QUAD and QUAD % blk_dev == 0 and rows % QUAD == 0 and group % 8 == 0
    following = passed_along(dense, "gx", -1)
    if fits and orbs % LANES == LANES // 2 and orbs % (4 * QUAD * QUAD) == 0:
        own, send, packed = first_turned(target, rounded, exchanged(pack(edge_tiles, 0, orbs)), rows)
        arrive = passed_along(send, "gx", 1)
        owned = unpack(packed, rows, orbs, orbs)
    else:
        owned = lax.all_to_all(edge_tiles, "gx", split_axis=0, concat_axis=1, tiled=True)
        own, send = turned_terms(target, rounded, owned)
        arrive = passed_along(send, "gx", 1)
    direct = direct_terms(target, rounded, following, own, owned, dot_nt)
    mirror = mirrored(owned, direct)
    previous = trial_panel
    current, rounded, dense = updated(direct, arrive)
    for k in range(1, DEGREE):
        following = passed_along(dense, "gx", -1)
        own, send = turned_terms(target, rounded, owned)
        arrive = passed_along(send, "gx", 1)
        direct = direct_terms(target, rounded, following, own, mirror, dot_nn)
        if k == DEGREE - 1:
            total = final_update(direct, arrive, previous)
        elif k == DEGREE - 2:
            rounded, dense = updated(direct, arrive, previous, total=False)
            direct, arrive, previous, rounded, dense = lax.optimization_barrier(
                (direct, arrive, previous, rounded, dense)
            )
            (total,) = updated(direct, arrive, previous, rounded=False)
        else:
            total, rounded, dense = updated(direct, arrive, previous)
        previous, current = current, total
    return previous, current


def solution(mesh):
    return jax.shard_map(
        per_device,
        mesh=mesh,
        in_specs=(P("member", "gx", None), P(("member", "gx"), None, None), P()),
        out_specs=(P(("member", "gx"), None, None), P(("member", "gx"), None, None)),
        check_vma=False,
    )
```
